32 devices in a mesh: groups: 2 (over y), mp: 4 (over z), dp: 2 (over x), rep: 2 (over core).
Axes of the slice: x: 2, y: 2, z: 4, core: 2. Of those that a mesh axis runs over, the one named last changes fastest.
Arguments:
- activations: bfloat16 [2048, 2048], P(('groups', 'dp', 'rep'), 'mp'), parts along dimension 0, may hold values from -6 to 6
- out_grads: bfloat16 [2048, 7168], P(('groups', 'dp', 'rep'), 'mp'), parts along dimension 0, may hold values from -6 to 6
- basis_grad: bfloat16 [14336, 7168], P(('groups', 'mp'), ('dp', 'rep')), parts along dimension 0, may hold values from -0.0625 to 0.0625
- basis_act: bfloat16 [4096, 2048], P(('groups', 'dp', 'rep'), 'mp'), parts along dimension 0, may hold values from -0.125 to 0.125
- eigen_values: float32 [14336, 2048], P(('groups', 'dp', 'rep'), 'mp'), parts along dimension 0, may hold values from 0.5 to 16
- token_counts: int32 [64], P(('groups', 'dp', 'rep')), parts along dimension 0, may hold values from 16 to 32
- fail_ids: int32 [48], P('groups'), parts along dimension 0, may hold values from 0 to 31, as said below
Outputs:
- preconditioned: float32 [14336, 2048], P(('groups', 'mp'), ('dp', 'rep')), parts along dimension 0
The draws below stay inside these ranges and needn't reach their ends.
There are 2 independent parts, one for each index of `groups`. The reference program is written for one: setup_inputs(seed, part) draws one part's arguments, and reference() takes and returns one part's arrays. A program takes and returns all parts, laid end to end along the dimension named above; each array names one. Nothing has to cross between parts.
Inputs may be any that keep to these rules, and one draw needn't show every extreme that they name: `fail_ids`: 24 distinct prompt indices.
All inputs are finite; a program needn't handle non-finite values.
Results may differ from the reference program's by a relative error of at most 0.015.
Values may be sent and summed in bfloat16 or wider, within the bound.
A program may use at most 128 MiB of HBM per device.

```python
import math
import jax
import jax.numpy as jnp
from jax import lax

D = 2048
FF = 7168
LEN = 32
TOKENS = 1024
POOL = 32
FAIL = 24
N_MP = 4
N_DP = 2
N_REP = 2


def draw_fail_ids(key, part):
    key = jax.random.fold_in(key, 7)
    shuffled = jax.random.permutation(key, POOL)
    return shuffled[:FAIL].astype(jnp.int32)


def plant(result, key, least, high):
    extent = result.shape
    place = [jax.random.randint(jax.random.fold_in(key, axis), (), 0, extent[axis]) for axis in range(len(extent))]
    result = result.at[tuple(place)].set(least)
    longest = extent.index(max(extent))
    place[longest] = (place[longest] + 1) % extent[longest]
    return result.at[tuple(place)].set(high)


def block_levels(own_key, extent, shards, smallest, high):
    level, own = 1.0, jax.random.fold_in(own_key, 6)
    for position, blocks in shards:
        draws = jnp.exp(jax.random.uniform(jax.random.fold_in(own, position), (blocks,), jnp.float32, smallest / len(shards), high / len(shards)))
        level = level * jnp.repeat(draws, extent[position] // blocks).reshape([-1 if axis == position else 1 for axis in range(len(extent))])
    return level


def gaussian(own_key, shape, scale, reach, pieces=(), kind=jnp.bfloat16):
    level = block_levels(own_key, shape, pieces, -0.22, 0.18) if pieces else 1.0
    entries = jax.random.normal(own_key, shape, jnp.float32) * scale * level
    return jnp.minimum(jnp.maximum(entries, -reach), reach).astype(kind)


def setup_inputs(seed: int = 0, part: int = 0) -> dict:
    arg_keys = jax.random.split(jax.random.key(seed), 8)
    part_keys = jax.random.split(jax.random.fold_in(arg_keys[7], part), 8)
    activations = gaussian(part_keys[0], (TOKENS, D), 1.0, 6.0, ((0, 4), (1, 4)))
    out_grads = gaussian(part_keys[1], (TOKENS, FF), 1.0, 6.0, ((0, 4), (1, 4)))
    basis_grad = gaussian(part_keys[2], (FF, FF), FF ** -0.5, 0.0625, ((0, 4), (1, 4)))
    basis_act = gaussian(part_keys[3], (D, D), D ** -0.5, 0.125, ((0, 4), (1, 4)))
    eigen_values = jnp.clip(jnp.exp(math.log(16.0) - 3.465736 * jax.random.uniform(part_keys[4], (FF, D), jnp.float32) ** block_levels(part_keys[4], (FF, D), ((0, 4), (1, 4)), -0.2, 0.2)), 0.5, 16.0)
    token_counts = plant(jax.random.randint(part_keys[5], (POOL,), LEN // 2, LEN + 1), jax.random.fold_in(part_keys[5], 1), LEN // 2, LEN).astype(jnp.int32)
    fail_ids = draw_fail_ids(jax.random.fold_in(jax.random.fold_in(arg_keys[7], part), 71), part)
    return {"activations": activations, "out_grads": out_grads, "basis_grad": basis_grad, "basis_act": basis_act, "eigen_values": eigen_values, "token_counts": token_counts, "fail_ids": fail_ids}


DAMPING = 0.25


def reference(activations, out_grads, basis_grad, basis_act, eigen_values, token_counts, fail_ids):
    chosen = jnp.any(jnp.arange(POOL, dtype=jnp.int32)[:, None] == fail_ids[None, :], axis=1)
    live_slot = jnp.arange(LEN, dtype=jnp.int32)[None, :] < token_counts[:, None]
    inverse = 1.0 / token_counts.astype(jnp.float32)
    weight = jnp.where(live_slot & chosen[:, None], inverse[:, None], jnp.float32(0.0)).astype(jnp.float32).reshape(TOKENS)
    scaled_grads = (out_grads.astype(jnp.float32) * weight[:, None]).astype(jnp.bfloat16)
    rotated_acts = jnp.dot(activations, basis_act, preferred_element_type=jnp.float32).astype(jnp.bfloat16)
    data_blocks = N_DP * N_REP
    token_block = TOKENS // data_blocks

    def token_step(carry, index):
        grads_part = lax.dynamic_slice_in_dim(scaled_grads, index * token_block, token_block, 0)
        acts_part = lax.dynamic_slice_in_dim(rotated_acts, index * token_block, token_block, 0)
        partial_value = lax.dot_general(grads_part, acts_part, (((0,), (0,)), ((), ())), preferred_element_type=jnp.float32)
        return carry + partial_value.astype(jnp.bfloat16).astype(jnp.float32), None

    total, unused = lax.scan(token_step, jnp.zeros((FF, D), jnp.float32), jnp.arange(data_blocks, dtype=jnp.int32))
    half_rotated = total.astype(jnp.bfloat16)
    row_block = FF // N_MP

    def eigen_step(carry, index):
        basis_part = lax.dynamic_slice_in_dim(basis_grad, index * row_block, row_block, 0)
        grad_part = lax.dynamic_slice_in_dim(half_rotated, index * row_block, row_block, 0)
        partial_value = lax.dot_general(basis_part, grad_part, (((0,), (0,)), ((), ())), preferred_element_type=jnp.float32)
        return carry + partial_value.astype(jnp.bfloat16).astype(jnp.float32), None

    eigen_grad, unused = lax.scan(eigen_step, jnp.zeros((FF, D), jnp.float32), jnp.arange(N_MP, dtype=jnp.int32))
    damped = (eigen_grad / (eigen_values + DAMPING)).astype(jnp.bfloat16)
    col_block = FF // data_blocks

    def back_step(carry, index):
        basis_part = lax.dynamic_slice_in_dim(basis_grad, index * col_block, col_block, 1)
        damped_part = lax.dynamic_slice_in_dim(damped, index * col_block, col_block, 0)
        partial_value = jnp.dot(basis_part, damped_part, preferred_element_type=jnp.float32)
        return carry + partial_value.astype(jnp.bfloat16).astype(jnp.float32), None

    back_sum, unused = lax.scan(back_step, jnp.zeros((FF, D), jnp.float32), jnp.arange(data_blocks, dtype=jnp.int32))
    back_rotated = back_sum.astype(jnp.bfloat16)
    return lax.dot_general(back_rotated, basis_act, (((1,), (1,)), ((), ())), preferred_element_type=jnp.float32)
```

```python
import functools

import jax
import jax.numpy as jnp
from jax import lax
from jax.experimental import pallas as pl
from jax.experimental.pallas import tpu as pltpu
from jax.sharding import PartitionSpec as P

LEN = 32
DAMPING = 0.25
STEPS = 16
MESH = pl.DeviceIdType.MESH
VMEM_LIMIT = 60 * 1024 * 1024


def remote(src, dst, send, recv, where):
    return pltpu.make_async_remote_copy(
        src_ref=src, dst_ref=dst, send_sem=send, recv_sem=recv, device_id=where, device_id_type=MESH
    )


def when(there, act):
    if there is True:
        act()
    else:
        pl.when(there)(act)


def z_links(n_mp):
    z = lax.axis_index("mp")
    return [(z > 0, {"mp": z - 1}), (z < n_mp - 1, {"mp": z + 1})]


def x_links(n_dp):
    x = lax.axis_index("dp")
    return [(True, {"dp": lax.rem(x + i, n_dp)}) for i in range(1, n_dp)]


def core_links(n_rep):
    c = lax.axis_index("rep")
    return [(True, {"rep": lax.rem(c + i, n_rep)}) for i in range(1, n_rep)]


def greet(links):
    barrier = pltpu.get_barrier_semaphore()
    for there, where in links:
        when(there, lambda where=where: pl.semaphore_signal(
            barrier, inc=1, device_id=where, device_id_type=MESH))
    pl.semaphore_wait(barrier, sum(1 if there is True else there.astype(jnp.int32) for there, _ in links))


class PlaneGather:
    def __init__(self, src, buf, send, recv, n_dp, n_rep):
        self.src, self.buf, self.send, self.recv = src, buf, send, recv
        self.n_dp, self.n_rep = n_dp, n_rep
        self.rows = src.shape[0]
        self.x, self.c = lax.axis_index("dp"), lax.axis_index("rep")
        self.k = self.x * n_rep + self.c

    def slot(self, k):
        return self.buf.at[pl.ds(pl.multiple_of(k * self.rows, self.rows), self.rows)]

    def first(self):
        out = []
        for n, where in enumerate(w for _, w in x_links(self.n_dp) + core_links(self.n_rep)):
            out.append(remote(self.src, self.slot(self.k), self.send.at[n], self.recv.at[self.k], where))
        return out

    def second(self):
        out = []
        n = self.n_dp + self.n_rep - 2
        for i in range(1, self.n_dp):
            k = lax.rem(self.x + i, self.n_dp) * self.n_rep + self.c
            group = []
            for _, where in core_links(self.n_rep):
                group.append(remote(self.slot(k), self.slot(k), self.send.at[n], self.recv.at[k], where))
                n += 1
            out.append((k, group))
        return out

    def arrive(self, k):
        remote(self.slot(k), self.slot(k), self.send.at[0], self.recv.at[k], {"rep": self.c}).wait_recv()

    def start(self):
        for copy in self.first():
            copy.start()

    def forward(self):
        for k, group in self.second():
            self.arrive(k)
            for copy in group:
                copy.start()

    def finish(self):
        for i in range(self.n_dp):
            for j in range(1, self.n_rep):
                self.arrive(lax.rem(self.x + i, self.n_dp) * self.n_rep + lax.rem(self.c + j, self.n_rep))
        self.slot(self.k)[...] = self.src[...]
        for copy in self.first():
            copy.wait_send()
        for _, group in self.second():
            for copy in group:
                copy.wait_send()


class LineGather:
    def __init__(self, buf, parts, send, recv, n_mp):
        self.buf, self.parts, self.send, self.recv, self.n_mp = buf, parts, send, recv, n_mp
        self.z = lax.axis_index("mp")

    def copy(self, m, h, way):
        i = m * self.parts + h
        return remote(self.buf.at[i], self.buf.at[i], self.send.at[way, i], self.recv.at[i],
                      {"mp": self.z + 2 * way - 1})

    def out(self, m, h, way, act):
        last = self.z < self.n_mp - 1 if way else self.z > 0

        @pl.when(last)
        def _():
            act(self.copy(m, h, way))

    def start(self):
        for h in range(self.parts):
            for way in (0, 1):
                self.out(self.z, h, way, lambda copy: copy.start())

    def take_left(self, m, h):
        self.copy(m, h, 1).wait_recv()
        self.out(m, h, 1, lambda copy: copy.start())

    def take_right(self, m, h):
        self.copy(m, h, 0).wait_recv()
        self.out(m, h, 0, lambda copy: copy.start())

    def step(self, s):
        for h in range(self.parts):
            @pl.when(self.z - s >= 0)
            def _():
                self.take_left(self.z - s, h)

            @pl.when(self.z + s < self.n_mp)
            def _():
                self.take_right(self.z + s, h)

    def finish(self):
        @pl.loop(0, self.n_mp)
        def _(m):
            for h in range(self.parts):
                @pl.when(m <= self.z)
                def _():
                    self.out(m, h, 1, lambda copy: copy.wait_send())

                @pl.when(m >= self.z)
                def _():
                    self.out(m, h, 0, lambda copy: copy.wait_send())


def gather_kernel(n_mp, n_dp, n_rep, fails, ids, s_ref, a_ref, q_ref, s_out, r_out, q_out,
                  s_all, a_all, q_rows, q_cols, r_own, r_all,
                  s_send, s_recv, a_send, a_recv, qr_send, qr_recv, qc_send, qc_recv, r_send, r_recv):
    z = lax.axis_index("mp")
    greet(z_links(n_mp) + x_links(n_dp) + core_links(n_rep))
    s = PlaneGather(s_ref, s_all, s_send, s_recv, n_dp, n_rep)
    qc = PlaneGather(q_ref, q_cols, qc_send, qc_recv, n_dp, n_rep)
    r = PlaneGather(r_own, r_all, r_send, r_recv, n_dp, n_rep)
    a = LineGather(a_all, 1, a_send, a_recv, n_mp)
    qr = LineGather(q_rows, 1, qr_send, qr_recv, n_mp)
    s.start()
    a_all[z] = a_ref[...]
    a.start()
    qc.start()
    q_rows[z] = q_ref[...]
    qr.start()
    for i in range(1, n_mp):
        a.step(i)
    s.forward()
    qc.forward()
    qc.finish()
    depth = a_ref.shape[1]

    total = jnp.zeros((a_ref.shape[0], q_ref.shape[1]), jnp.float32)
    total = lax.fori_loop(
        0, n_mp,
        lambda m, t: t + jnp.dot(a_all[m], q_cols[pl.ds(pl.multiple_of(m * depth, depth), depth), :],
                                 preferred_element_type=jnp.float32),
        total)
    r_own[...] = total.astype(jnp.bfloat16).reshape(r_own.shape)
    r.start()
    s.finish()

    @pl.loop(0, fails)
    def _(i):
        s_out[i] = s_all[ids[i]]

    r.forward()
    r.finish()

    @pl.loop(0, fails)
    def _(i):
        r_out[i] = r_all[ids[i]]

    for i in range(1, n_mp):
        qr.step(i)
    width = q_ref.shape[1]

    @pl.loop(0, n_mp)
    def _(m):
        q_out[:, pl.ds(pl.multiple_of(m * width, width), width)] = q_rows[m]

    a.finish()
    qr.finish()


def sum_kernel(n_mp, u_ref, out_ref, left, right, l_send, l_recv, r_send, r_recv):
    z = lax.axis_index("mp")
    greet(z_links(n_mp))
    rows = u_ref.shape[0] // STEPS

    def at(i):
        return pl.ds(pl.multiple_of(i * rows, rows), rows)

    def copy(buf, i, send, recv, way):
        return remote(buf.at[at(i)], buf.at[at(i)], send.at[i], recv.at[i], {"mp": z + way})

    def take(buf, i, send, recv, way, first, last):
        @pl.when(first)
        def _():
            buf[at(i), :] = u_ref[at(i), :]

        @pl.when(jnp.logical_not(first))
        def _():
            copy(buf, i, send, recv, way).wait_recv()
            buf[at(i), :] = (buf[at(i), :].astype(jnp.float32)
                             + u_ref[at(i), :].astype(jnp.float32)).astype(jnp.bfloat16)

        @pl.when(jnp.logical_not(last))
        def _():
            copy(buf, i, send, recv, way).start()

    @pl.loop(0, STEPS + n_mp - 1)
    def _(t):
        i = t - z
        j = t - (n_mp - 1 - z)

        @pl.when((i >= 0) & (i < STEPS))
        def _():
            take(left, i, l_send, l_recv, 1, z == 0, z == n_mp - 1)

        @pl.when((j >= 0) & (j < STEPS))
        def _():
            take(right, j, r_send, r_recv, -1, z == n_mp - 1, z == 0)

    @pl.loop(0, STEPS)
    def _(i):
        out_ref[at(i), :] = (left[at(i), :].astype(jnp.float32) + right[at(i), :].astype(jnp.float32)
                             - u_ref[at(i), :].astype(jnp.float32)).astype(jnp.bfloat16)

        @pl.when(z < n_mp - 1)
        def _():
            copy(left, i, l_send, l_recv, 1).wait_send()

        @pl.when(z > 0)
        def _():
            copy(right, i, r_send, r_recv, -1).wait_send()


def back_kernel(n_mp, n_dp, n_rep, parts, d_ref, g_ref, out_ref, held, part, other, across,
                z_send, z_recv, c_send, c_recv, x_send, x_recv, o_send, o_recv):
    z, x, c = lax.axis_index("mp"), lax.axis_index("dp"), lax.axis_index("rep")
    greet(z_links(n_mp) + x_links(n_dp) + core_links(n_rep))
    n = n_mp * parts
    rows, width = held.shape[1], held.shape[2]
    half = rows // n_rep
    tile = next(t for t in (256, 128, 64, 32, 16) if rows % t == 0)
    small = next(t for t in (128, 64, 32, 16) if half % t == 0)
    core = {"rep": 1 - c}
    mine = pl.ds(pl.multiple_of(c * half, half), half)
    theirs = pl.ds(pl.multiple_of((1 - c) * half, half), half)
    line = LineGather(held, parts, z_send, z_recv, n_mp)

    for h in range(parts):
        held[z * parts + h] = d_ref[:, h * width:(h + 1) * width]
    line.start()

    low, high = z, n_mp - 1 - z
    near = jnp.minimum(low, high)
    both = 2 * near * parts

    def place(p):
        q = p - parts
        pair, turn = q // (2 * parts), q % (2 * parts)
        far = q - both
        is_pair = q < both
        s = jnp.where(is_pair, pair + 1, near + far // parts + 1)
        h = jnp.where(is_pair, turn // 2, far % parts)
        from_left = jnp.where(is_pair, turn % 2 == 0, low > high)
        own = p < parts
        m = jnp.where(own, z, jnp.where(from_left, z - s, z + s))
        return m, jnp.where(own, p, h), own, from_left

    def columns(p):
        m, h, _, _ = place(p)
        return pl.ds(pl.multiple_of((m * parts + h) * width, width), width)

    def core_copy(p):
        return remote(part.at[p, theirs], other.at[p], c_send.at[p], c_recv.at[p], core)

    def x_copies(p):
        return [remote(part.at[p, mine], across.at[p, i - 1], x_send.at[p, i - 1], x_recv.at[p, i - 1],
                       {"dp": lax.rem(x + i, n_dp)}) for i in range(1, n_dp)]

    def out_copy(p, whose):
        return remote(out_ref.at[whose, columns(p)], out_ref.at[whose, columns(p)], o_send.at[p], o_recv.at[p], core)

    def multiply(p):
        m, h, own, from_left = place(p)

        @pl.when(jnp.logical_not(own) & from_left)
        def _():
            line.take_left(m, h)

        @pl.when(jnp.logical_not(own) & jnp.logical_not(from_left))
        def _():
            line.take_right(m, h)

        @pl.loop(0, rows // tile)
        def _(t):
            at = pl.ds(pl.multiple_of(t * tile, tile), tile)
            part[p, at, :] = jnp.dot(
                g_ref[at, :], held[m * parts + h], preferred_element_type=jnp.float32).astype(jnp.bfloat16)

        core_copy(p).start()

    def add_cores(p):
        core_copy(p).wait()

        @pl.loop(0, half // small)
        def _(t):
            here = pl.ds(pl.multiple_of(c * half + t * small, small), small)
            at = pl.ds(pl.multiple_of(t * small, small), small)
            part[p, here, :] = (part[p, here, :].astype(jnp.float32)
                                + other[p, at, :].astype(jnp.float32)).astype(jnp.bfloat16)

        for copy in x_copies(p):
            copy.start()

    def add_chips(p):
        for copy in x_copies(p):
            copy.wait()

        @pl.loop(0, half // small)
        def _(t):
            here = pl.ds(pl.multiple_of(c * half + t * small, small), small)
            at = pl.ds(pl.multiple_of(t * small, small), small)
            total = part[p, here, :].astype(jnp.float32)
            for i in range(n_dp - 1):
                total += across[p, i, at, :].astype(jnp.float32)
            out_ref[here, columns(p)] = total.astype(jnp.bfloat16)

        out_copy(p, mine).start()

    @pl.loop(0, n + 2)
    def _(t):
        @pl.when(t < n)
        def _():
            multiply(t)

        @pl.when((t >= 1) & (t < n + 1))
        def _():
            add_cores(t - 1)

        @pl.when(t >= 2)
        def _():
            add_chips(t - 2)

    @pl.loop(0, n)
    def _(p):
        out_copy(p, mine).wait_send()
        out_copy(p, theirs).wait_recv()

    line.finish()


def shards(n_mp, n_dp, n_rep, activations, out_grads, basis_grad, basis_act, eigen_values, token_counts, fail_ids):
    tokens, features = activations.shape
    hidden = out_grads.shape[1]
    wide = basis_grad.shape[1]
    rows = basis_act.shape[0]
    planes = n_dp * n_rep
    fails = fail_ids.shape[0]
    prompts = token_counts.shape[0]
    live = fails * LEN
    bf16 = jnp.bfloat16
    dma = pltpu.SemaphoreType.DMA
    vmem = pl.BlockSpec(memory_space=pltpu.VMEM)
    live_slot = jnp.arange(LEN, dtype=jnp.int32)[None, :] < token_counts[:, None]
    inverse = 1.0 / token_counts.astype(jnp.float32)
    weight = jnp.where(live_slot, inverse[:, None], jnp.float32(0.0)).reshape(tokens)
    scaled = (out_grads.astype(jnp.float32) * weight[:, None]).astype(bf16)

    sends = n_dp + n_rep - 2 + (n_dp - 1) * (n_rep - 1)
    plane_sems = [dma((sends,)), dma((planes,))]
    line_sems = [dma((2, n_mp)), dma((n_mp,))]
    grads, rotated, basis_rows = pl.pallas_call(
        functools.partial(gather_kernel, n_mp, n_dp, n_rep, fails),
        out_shape=(
            jax.ShapeDtypeStruct((fails, LEN, hidden), bf16),
            jax.ShapeDtypeStruct((fails, LEN, features), bf16),
            jax.ShapeDtypeStruct((rows, n_mp * features), bf16),
        ),
        in_specs=[pl.BlockSpec(memory_space=pltpu.SMEM), vmem, vmem, vmem],
        out_specs=(vmem, vmem, vmem),
        scratch_shapes=[
            pltpu.VMEM((planes * prompts, LEN, hidden), bf16),
            pltpu.VMEM((n_mp, tokens, features), bf16),
            pltpu.VMEM((n_mp, rows, features), bf16),
            pltpu.VMEM((planes * rows, features), bf16),
            pltpu.VMEM((prompts, LEN, features), bf16),
            pltpu.VMEM((planes * prompts, LEN, features), bf16),
        ] + plane_sems + line_sems + line_sems + plane_sems + plane_sems,
        compiler_params=pltpu.CompilerParams(
            collective_id=0, has_side_effects=True, vmem_limit_bytes=VMEM_LIMIT),
        name="gather_inputs",
    )(fail_ids, scaled.reshape(prompts, LEN, hidden), activations, basis_act)

    grads, rotated = grads.reshape(live, hidden), rotated.reshape(live, features)
    partial_u = jnp.dot(grads, basis_grad, preferred_element_type=jnp.float32).astype(bf16)
    turned = pl.pallas_call(
        functools.partial(sum_kernel, n_mp),
        out_shape=jax.ShapeDtypeStruct((live, wide), bf16),
        in_specs=[vmem],
        out_specs=vmem,
        scratch_shapes=[
            pltpu.VMEM((live, wide), bf16),
            pltpu.VMEM((live, wide), bf16),
        ] + [dma((STEPS,))] * 4,
        compiler_params=pltpu.CompilerParams(
            collective_id=1, has_side_effects=True, vmem_limit_bytes=VMEM_LIMIT),
        name="sum_turned",
    )(partial_u)

    eigen_grad = lax.dot_general(
        turned, rotated, (((0,), (0,)), ((), ())), preferred_element_type=jnp.float32)
    damped = (eigen_grad / (eigen_values + DAMPING)).astype(bf16)

    parts = max(1, features // 256)
    width = features // parts
    n = n_mp * parts
    half = hidden // n_rep
    back = pl.pallas_call(
        functools.partial(back_kernel, n_mp, n_dp, n_rep, parts),
        out_shape=jax.ShapeDtypeStruct((hidden, n_mp * features), bf16),
        in_specs=[vmem, vmem],
        out_specs=vmem,
        scratch_shapes=[
            pltpu.VMEM((n, wide, width), bf16),
            pltpu.VMEM((n, hidden, width), bf16),
            pltpu.VMEM((n, half, width), bf16),
            pltpu.VMEM((n, n_dp - 1, half, width), bf16),
            dma((2, n)), dma((n,)),
            dma((n,)), dma((n,)),
            dma((n, n_dp - 1)), dma((n, n_dp - 1)),
            dma((n,)), dma((n,)),
        ],
        compiler_params=pltpu.CompilerParams(
            collective_id=2, has_side_effects=True, vmem_limit_bytes=VMEM_LIMIT),
        name="back_rotate",
    )(damped, basis_grad)
    return lax.dot_general(
        back, basis_rows, (((1,), (1,)), ((), ())), preferred_element_type=jnp.float32)


def solution(mesh):
    return jax.shard_map(
        functools.partial(shards, mesh.shape["mp"], mesh.shape["dp"], mesh.shape["rep"]),
        mesh=mesh,
        in_specs=(
            P(("groups", "dp", "rep"), "mp"),
            P(("groups", "dp", "rep"), "mp"),
            P(("groups", "mp"), ("dp", "rep")),
            P(("groups", "dp", "rep"), "mp"),
            P(("groups", "dp", "rep"), "mp"),
            P(("groups", "dp", "rep")),
            P("groups"),
        ),
        out_specs=P(("groups", "mp"), ("dp", "rep")),
        check_vma=False,
    )
```

```python
import functools

import jax
import jax.numpy as jnp
from jax import lax
from jax.experimental import pallas as pl
from jax.experimental.pallas import tpu as pltpu
from jax.sharding import PartitionSpec as P

LEN = 32
DAMPING = 0.25
STEPS = 16
MESH = pl.DeviceIdType.MESH
VMEM_LIMIT = 60 * 1024 * 1024


def remote(src, dst, send, recv, where):
    return pltpu.make_async_remote_copy(
        src_ref=src, dst_ref=dst, send_sem=send, recv_sem=recv, device_id=where, device_id_type=MESH
    )


def when(there, act):
    if there is True:
        act()
    else:
        pl.when(there)(act)


def z_links(n_mp):
    z = lax.axis_index("mp")
    return [(z > 0, {"mp": z - 1}), (z < n_mp - 1, {"mp": z + 1})]


def x_links(n_dp):
    x = lax.axis_index("dp")
    return [(True, {"dp": lax.rem(x + i, n_dp)}) for i in range(1, n_dp)]


def core_links(n_rep):
    c = lax.axis_index("rep")
    return [(True, {"rep": lax.rem(c + i, n_rep)}) for i in range(1, n_rep)]


def greet(links):
    barrier = pltpu.get_barrier_semaphore()
    for there, where in links:
        when(there, lambda where=where: pl.semaphore_signal(
            barrier, inc=1, device_id=where, device_id_type=MESH))
    pl.semaphore_wait(barrier, sum(1 if there is True else there.astype(jnp.int32) for there, _ in links))


class PlaneGather:
    def __init__(self, src, buf, send, recv, n_dp, n_rep):
        self.src, self.buf, self.send, self.recv = src, buf, send, recv
        self.n_dp, self.n_rep = n_dp, n_rep
        self.rows = src.shape[0]
        self.x, self.c = lax.axis_index("dp"), lax.axis_index("rep")
        self.k = self.x * n_rep + self.c

    def slot(self, k):
        return self.buf.at[pl.ds(pl.multiple_of(k * self.rows, self.rows), self.rows)]

    def first(self):
        out = []
        for n, where in enumerate(w for _, w in x_links(self.n_dp) + core_links(self.n_rep)):
            out.append(remote(self.src, self.slot(self.k), self.send.at[n], self.recv.at[self.k], where))
        return out

    def second(self):
        out = []
        n = self.n_dp + self.n_rep - 2
        for i in range(1, self.n_dp):
            k = lax.rem(self.x + i, self.n_dp) * self.n_rep + self.c
            group = []
            for _, where in core_links(self.n_rep):
                group.append(remote(self.slot(k), self.slot(k), self.send.at[n], self.recv.at[k], where))
                n += 1
            out.append((k, group))
        return out

    def arrive(self, k):
        remote(self.slot(k), self.slot(k), self.send.at[0], self.recv.at[k], {"rep": self.c}).wait_recv()

    def start(self):
        for copy in self.first():
            copy.start()

    def forward(self):
        for k, group in self.second():
            self.arrive(k)
            for copy in group:
                copy.start()

    def finish(self):
        for i in range(self.n_dp):
            for j in range(1, self.n_rep):
                self.arrive(lax.rem(self.x + i, self.n_dp) * self.n_rep + lax.rem(self.c + j, self.n_rep))
        self.slot(self.k)[...] = self.src[...]
        for copy in self.first():
            copy.wait_send()
        for _, group in self.second():
            for copy in group:
                copy.wait_send()


class LineGather:
    def __init__(self, buf, parts, send, recv, n_mp):
        self.buf, self.parts, self.send, self.recv, self.n_mp = buf, parts, send, recv, n_mp
        self.z = lax.axis_index("mp")

    def copy(self, m, h, way):
        i = m * self.parts + h
        return remote(self.buf.at[i], self.buf.at[i], self.send.at[way, i], self.recv.at[i],
                      {"mp": self.z + 2 * way - 1})

    def out(self, m, h, way, act):
        last = self.z < self.n_mp - 1 if way else self.z > 0

        @pl.when(last)
        def _():
            act(self.copy(m, h, way))

    def start(self):
        for h in range(self.parts):
            for way in (0, 1):
                self.out(self.z, h, way, lambda copy: copy.start())

    def take_left(self, m, h):
        self.copy(m, h, 1).wait_recv()
        self.out(m, h, 1, lambda copy: copy.start())

    def take_right(self, m, h):
        self.copy(m, h, 0).wait_recv()
        self.out(m, h, 0, lambda copy: copy.start())

    def step(self, s):
        for h in range(self.parts):
            @pl.when(self.z - s >= 0)
            def _():
                self.take_left(self.z - s, h)

            @pl.when(self.z + s < self.n_mp)
            def _():
                self.take_right(self.z + s, h)

    def finish(self):
        @pl.loop(0, self.n_mp)
        def _(m):
            for h in range(self.parts):
                @pl.when(m <= self.z)
                def _():
                    self.out(m, h, 1, lambda copy: copy.wait_send())

                @pl.when(m >= self.z)
                def _():
                    self.out(m, h, 0, lambda copy: copy.wait_send())


def turn_kernel(n_mp, n_dp, n_rep, fails, ids, counts, g_ref, a_ref, q_ref, basis_ref, u_out, r_out, q_out,
                s_own, s_all, s_block, a_all, q_rows, q_cols, r_own, r_all, u_own, left, right,
                s_send, s_recv, a_send, a_recv, qr_send, qr_recv, qc_send, qc_recv, r_send, r_recv,
                ul_send, ul_recv, ur_send, ur_recv):
    z = lax.axis_index("mp")
    greet(z_links(n_mp) + x_links(n_dp) + core_links(n_rep))
    s = PlaneGather(s_own, s_all, s_send, s_recv, n_dp, n_rep)
    qc = PlaneGather(q_ref, q_cols, qc_send, qc_recv, n_dp, n_rep)
    r = PlaneGather(r_own, r_all, r_send, r_recv, n_dp, n_rep)
    a = LineGather(a_all, 1, a_send, a_recv, n_mp)
    qr = LineGather(q_rows, 1, qr_send, qr_recv, n_mp)
    depth, width = a_ref.shape[1], q_ref.shape[1]
    wide = basis_ref.shape[1]
    rows = u_own.shape[0] // STEPS
    blocks = u_own.shape[0] // (s_block.shape[0] * LEN)
    per = STEPS // blocks
    tile = 256 if wide % 256 == 0 else wide

    a_all[z] = a_ref[...]
    a.start()

    @pl.loop(0, counts.shape[0])
    def _(i):
        count = jnp.full((LEN, 1), counts[i], jnp.int32)
        slot = lax.broadcasted_iota(jnp.int32, (LEN, 1), 0)
        weight = jnp.where(slot < count, 1.0 / count.astype(jnp.float32), 0.0)
        s_own[i] = (g_ref[i].astype(jnp.float32) * weight).astype(jnp.bfloat16)

    s.start()
    q_rows[z] = q_ref[...]
    a.step(1)
    qr.start()
    for i in range(2, n_mp):
        a.step(i)
    s.forward()
    qc.start()
    s.finish()

    def at(i):
        return pl.ds(pl.multiple_of(i * rows, rows), rows)

    def copy(buf, i, send, recv, way):
        return remote(buf.at[at(i)], buf.at[at(i)], send.at[i], recv.at[i], {"mp": z + way})

    def take(buf, i, send, recv, way, first, last):
        @pl.when(first)
        def _():
            buf[at(i), :] = u_own[at(i), :]

        @pl.when(jnp.logical_not(first))
        def _():
            copy(buf, i, send, recv, way).wait_recv()
            buf[at(i), :] = (buf[at(i), :].astype(jnp.float32)
                             + u_own[at(i), :].astype(jnp.float32)).astype(jnp.bfloat16)

        @pl.when(jnp.logical_not(last))
        def _():
            copy(buf, i, send, recv, way).start()

    def turn(block):
        prompts = s_block.shape[0]

        @pl.loop(0, prompts)
        def _(i):
            s_block[i] = s_all[ids[block * prompts + i]]

        size = prompts * LEN
        here = pl.ds(pl.multiple_of(block * size, size), size)

        @pl.loop(0, wide // tile)
        def _(j):
            cols = pl.ds(pl.multiple_of(j * tile, tile), tile)
            u_own[here, cols] = jnp.dot(
                s_block[...].reshape(size, s_block.shape[2]), basis_ref[:, cols],
                preferred_element_type=jnp.float32).astype(jnp.bfloat16)

    def rotate():
        qc.finish()
        total = jnp.zeros((a_ref.shape[0], width), jnp.float32)
        total = lax.fori_loop(
            0, n_mp,
            lambda m, t: t + jnp.dot(a_all[m], q_cols[pl.ds(pl.multiple_of(m * depth, depth), depth), :],
                                     preferred_element_type=jnp.float32),
            total)
        r_own[...] = total.astype(jnp.bfloat16).reshape(r_own.shape)
        r.start()

    @pl.loop(0, STEPS + n_mp - 1)
    def _(t):
        @pl.when((t < STEPS) & (t % per == 0))
        def _():
            turn(t // per)

        i = t - z
        j = t - (n_mp - 1 - z)

        @pl.when((i >= 0) & (i < STEPS))
        def _():
            take(left, i, ul_send, ul_recv, 1, z == 0, z == n_mp - 1)

        @pl.when((j >= 0) & (j < STEPS))
        def _():
            take(right, j, ur_send, ur_recv, -1, z == n_mp - 1, z == 0)

        for n in range(1, n_mp):
            @pl.when(t == (n - 1) * STEPS // (n_mp - 1))
            def _():
                qr.step(n)

        @pl.when(t == STEPS // 2)
        def _():
            qc.forward()

        @pl.when(t == 3 * STEPS // 4)
        def _():
            rotate()

        @pl.when(t == STEPS)
        def _():
            r.forward()

    @pl.loop(0, STEPS)
    def _(i):
        u_out[at(i), :] = (left[at(i), :].astype(jnp.float32) + right[at(i), :].astype(jnp.float32)
                           - u_own[at(i), :].astype(jnp.float32)).astype(jnp.bfloat16)

        @pl.when(z < n_mp - 1)
        def _():
            copy(left, i, ul_send, ul_recv, 1).wait_send()

        @pl.when(z > 0)
        def _():
            copy(right, i, ur_send, ur_recv, -1).wait_send()

    r.finish()

    @pl.loop(0, fails)
    def _(i):
        r_out[i] = r_all[ids[i]]

    @pl.loop(0, n_mp)
    def _(m):
        q_out[:, pl.ds(pl.multiple_of(m * width, width), width)] = q_rows[m]

    a.finish()
    qr.finish()


def back_kernel(n_mp, n_dp, n_rep, parts, d_ref, g_ref, q_ref, out_ref, back, held, part, other, across,
                z_send, z_recv, c_send, c_recv, x_send, x_recv, o_send, o_recv):
    z, x, c = lax.axis_index("mp"), lax.axis_index("dp"), lax.axis_index("rep")
    greet(z_links(n_mp) + x_links(n_dp) + core_links(n_rep))
    n = n_mp * parts
    rows, width = held.shape[1], held.shape[2]
    half = rows // n_rep
    tile = next(t for t in (256, 128, 64, 32, 16) if rows % t == 0)
    small = next(t for t in (128, 64, 32, 16) if half % t == 0)
    core = {"rep": 1 - c}
    mine = pl.ds(pl.multiple_of(c * half, half), half)
    theirs = pl.ds(pl.multiple_of((1 - c) * half, half), half)
    line = LineGather(held, parts, z_send, z_recv, n_mp)

    for h in range(parts):
        held[z * parts + h] = d_ref[:, h * width:(h + 1) * width]
    line.start()

    low, high = z, n_mp - 1 - z
    near = jnp.minimum(low, high)
    both = 2 * near * parts

    def place(p):
        q = p - parts
        pair, turn = q // (2 * parts), q % (2 * parts)
        far = q - both
        is_pair = q < both
        s = jnp.where(is_pair, pair + 1, near + far // parts + 1)
        h = jnp.where(is_pair, turn // 2, far % parts)
        from_left = jnp.where(is_pair, turn % 2 == 0, low > high)
        own = p < parts
        m = jnp.where(own, z, jnp.where(from_left, z - s, z + s))
        return m, jnp.where(own, p, h), own, from_left

    def columns(p):
        m, h, _, _ = place(p)
        return pl.ds(pl.multiple_of((m * parts + h) * width, width), width)

    def core_copy(p):
        return remote(part.at[p, theirs], other.at[p], c_send.at[p], c_recv.at[p], core)

    def x_copies(p):
        return [remote(part.at[p, mine], across.at[p, i - 1], x_send.at[p, i - 1], x_recv.at[p, i - 1],
                       {"dp": lax.rem(x + i, n_dp)}) for i in range(1, n_dp)]

    def out_copy(p, whose):
        return remote(back.at[whose, columns(p)], back.at[whose, columns(p)], o_send.at[p], o_recv.at[p], core)

    def multiply(p):
        m, h, own, from_left = place(p)

        @pl.when(jnp.logical_not(own) & from_left)
        def _():
            line.take_left(m, h)

        @pl.when(jnp.logical_not(own) & jnp.logical_not(from_left))
        def _():
            line.take_right(m, h)

        @pl.loop(0, rows // tile)
        def _(t):
            at = pl.ds(pl.multiple_of(t * tile, tile), tile)
            part[p, at, :] = jnp.dot(
                g_ref[at, :], held[m * parts + h], preferred_element_type=jnp.float32).astype(jnp.bfloat16)

        core_copy(p).start()

    def add_cores(p):
        core_copy(p).wait()

        @pl.loop(0, half // small)
        def _(t):
            here = pl.ds(pl.multiple_of(c * half + t * small, small), small)
            at = pl.ds(pl.multiple_of(t * small, small), small)
            part[p, here, :] = (part[p, here, :].astype(jnp.float32)
                                + other[p, at, :].astype(jnp.float32)).astype(jnp.bfloat16)

        for copy in x_copies(p):
            copy.start()

    def add_chips(p):
        for copy in x_copies(p):
            copy.wait()

        @pl.loop(0, half // small)
        def _(t):
            here = pl.ds(pl.multiple_of(c * half + t * small, small), small)
            at = pl.ds(pl.multiple_of(t * small, small), small)
            total = part[p, here, :].astype(jnp.float32)
            for i in range(n_dp - 1):
                total += across[p, i, at, :].astype(jnp.float32)
            back[here, columns(p)] = total.astype(jnp.bfloat16)

        out_copy(p, mine).start()

    def finish(p):
        out_copy(p, theirs).wait_recv()
        cols = columns(p)

        @pl.loop(0, rows // tile)
        def _(t):
            at = pl.ds(pl.multiple_of(t * tile, tile), tile)
            out_ref[at, :] += lax.dot_general(
                back[at, cols], q_ref[:, cols], (((1,), (1,)), ((), ())), preferred_element_type=jnp.float32)

    out_ref[...] = jnp.zeros_like(out_ref)

    @pl.loop(0, n + 3)
    def _(t):
        @pl.when(t < n)
        def _():
            multiply(t)

        @pl.when((t >= 1) & (t < n + 1))
        def _():
            add_cores(t - 1)

        @pl.when((t >= 2) & (t < n + 2))
        def _():
            add_chips(t - 2)

        @pl.when(t >= 3)
        def _():
            finish(t - 3)

    @pl.loop(0, n)
    def _(p):
        out_copy(p, mine).wait_send()

    line.finish()


def shards(n_mp, n_dp, n_rep, activations, out_grads, basis_grad, basis_act, eigen_values, token_counts, fail_ids):
    tokens, features = activations.shape
    hidden = out_grads.shape[1]
    wide = basis_grad.shape[1]
    rows = basis_act.shape[0]
    planes = n_dp * n_rep
    fails = fail_ids.shape[0]
    prompts = token_counts.shape[0]
    live = fails * LEN
    bf16 = jnp.bfloat16
    dma = pltpu.SemaphoreType.DMA
    vmem = pl.BlockSpec(memory_space=pltpu.VMEM)
    sends = n_dp + n_rep - 2 + (n_dp - 1) * (n_rep - 1)
    plane_sems = [dma((sends,)), dma((planes,))]
    line_sems = [dma((2, n_mp)), dma((n_mp,))]
    smem = pl.BlockSpec(memory_space=pltpu.SMEM)
    blocks = next(b for b in (4, 2, 1) if fails % b == 0 and STEPS % b == 0)
    turned, rotated, basis_rows = pl.pallas_call(
        functools.partial(turn_kernel, n_mp, n_dp, n_rep, fails),
        out_shape=(
            jax.ShapeDtypeStruct((live, wide), bf16),
            jax.ShapeDtypeStruct((fails, LEN, features), bf16),
            jax.ShapeDtypeStruct((rows, n_mp * features), bf16),
        ),
        in_specs=[smem, smem, vmem, vmem, vmem, vmem],
        out_specs=(vmem, vmem, vmem),
        scratch_shapes=[
            pltpu.VMEM((prompts, LEN, hidden), bf16),
            pltpu.VMEM((planes * prompts, LEN, hidden), bf16),
            pltpu.VMEM((fails // blocks, LEN, hidden), bf16),
            pltpu.VMEM((n_mp, tokens, features), bf16),
            pltpu.VMEM((n_mp, rows, features), bf16),
            pltpu.VMEM((planes * rows, features), bf16),
            pltpu.VMEM((prompts, LEN, features), bf16),
            pltpu.VMEM((planes * prompts, LEN, features), bf16),
            pltpu.VMEM((live, wide), bf16),
            pltpu.VMEM((live, wide), bf16),
            pltpu.VMEM((live, wide), bf16),
        ] + plane_sems + line_sems + line_sems + plane_sems + plane_sems + [dma((STEPS,))] * 4,
        compiler_params=pltpu.CompilerParams(
            collective_id=0, has_side_effects=True, vmem_limit_bytes=VMEM_LIMIT),
        name="turn_grads",
    )(fail_ids, token_counts, out_grads.reshape(prompts, LEN, hidden), activations, basis_act, basis_grad)
    rotated = rotated.reshape(live, features)

    eigen_grad = lax.dot_general(
        turned, rotated, (((0,), (0,)), ((), ())), preferred_element_type=jnp.float32)
    damped = (eigen_grad / (eigen_values + DAMPING)).astype(bf16)

    parts = max(1, features // 256)
    width = features // parts
    n = n_mp * parts
    half = hidden // n_rep
    return pl.pallas_call(
        functools.partial(back_kernel, n_mp, n_dp, n_rep, parts),
        out_shape=jax.ShapeDtypeStruct((hidden, rows), jnp.float32),
        in_specs=[vmem, vmem, vmem],
        out_specs=vmem,
        scratch_shapes=[
            pltpu.VMEM((hidden, n_mp * features), bf16),
            pltpu.VMEM((n, wide, width), bf16),
            pltpu.VMEM((n, hidden, width), bf16),
            pltpu.VMEM((n, half, width), bf16),
            pltpu.VMEM((n, n_dp - 1, half, width), bf16),
            dma((2, n)), dma((n,)),
            dma((n,)), dma((n,)),
            dma((n, n_dp - 1)), dma((n, n_dp - 1)),
            dma((n,)), dma((n,)),
        ],
        compiler_params=pltpu.CompilerParams(
            collective_id=1, has_side_effects=True, vmem_limit_bytes=VMEM_LIMIT),
        name="back_rotate",
    )(damped, basis_grad, basis_rows)


def solution(mesh):
    return jax.shard_map(
        functools.partial(shards, mesh.shape["mp"], mesh.shape["dp"], mesh.shape["rep"]),
        mesh=mesh,
        in_specs=(
            P(("groups", "dp", "rep"), "mp"),
            P(("groups", "dp", "rep"), "mp"),
            P(("groups", "mp"), ("dp", "rep")),
            P(("groups", "dp", "rep"), "mp"),
            P(("groups", "dp", "rep"), "mp"),
            P(("groups", "dp", "rep")),
            P("groups"),
        ),
        out_specs=P(("groups", "mp"), ("dp", "rep")),
        check_vma=False,
    )
```

```python
import functools

import jax
import jax.numpy as jnp
from jax import lax
from jax.experimental import pallas as pl
from jax.experimental.pallas import tpu as pltpu
from jax.sharding import PartitionSpec as P

LEN = 32
DAMPING = 0.25
STEPS = 24
LAG = 2
MESH = pl.DeviceIdType.MESH
VMEM_LIMIT = 60 * 1024 * 1024


def remote(src, dst, send, recv, where):
    return pltpu.make_async_remote_copy(
        src_ref=src, dst_ref=dst, send_sem=send, recv_sem=recv, device_id=where, device_id_type=MESH
    )


def when(there, act):
    if there is True:
        act()
    else:
        pl.when(there)(act)


def z_links(n_mp):
    z = lax.axis_index("mp")
    return [(z > 0, {"mp": z - 1}), (z < n_mp - 1, {"mp": z + 1})]


def x_links(n_dp):
    x = lax.axis_index("dp")
    return [(True, {"dp": lax.rem(x + i, n_dp)}) for i in range(1, n_dp)]


def core_links(n_rep):
    c = lax.axis_index("rep")
    return [(True, {"rep": lax.rem(c + i, n_rep)}) for i in range(1, n_rep)]


def greet(links):
    barrier = pltpu.get_barrier_semaphore()
    for there, where in links:
        when(there, lambda where=where: pl.semaphore_signal(
            barrier, inc=1, device_id=where, device_id_type=MESH))
    pl.semaphore_wait(barrier, sum(1 if there is True else there.astype(jnp.int32) for there, _ in links))


class PlaneGather:
    def __init__(self, src, buf, send, recv, n_dp, n_rep):
        self.src, self.buf, self.send, self.recv = src, buf, send, recv
        self.n_dp, self.n_rep = n_dp, n_rep
        self.rows = src.shape[0]
        self.x, self.c = lax.axis_index("dp"), lax.axis_index("rep")
        self.k = self.x * n_rep + self.c

    def slot(self, k):
        return self.buf.at[pl.ds(pl.multiple_of(k * self.rows, self.rows), self.rows)]

    def first(self):
        out = []
        for n, where in enumerate(w for _, w in x_links(self.n_dp) + core_links(self.n_rep)):
            out.append(remote(self.src, self.slot(self.k), self.send.at[n], self.recv.at[self.k], where))
        return out

    def second(self):
        out = []
        n = self.n_dp + self.n_rep - 2
        for i in range(1, self.n_dp):
            k = lax.rem(self.x + i, self.n_dp) * self.n_rep + self.c
            group = []
            for _, where in core_links(self.n_rep):
                group.append(remote(self.slot(k), self.slot(k), self.send.at[n], self.recv.at[k], where))
                n += 1
            out.append((k, group))
        return out

    def arrive(self, k):
        remote(self.slot(k), self.slot(k), self.send.at[0], self.recv.at[k], {"rep": self.c}).wait_recv()

    def start(self):
        for copy in self.first():
            copy.start()

    def forward(self):
        for k, group in self.second():
            self.arrive(k)
            for copy in group:
                copy.start()

    def finish(self):
        for i in range(self.n_dp):
            for j in range(1, self.n_rep):
                self.arrive(lax.rem(self.x + i, self.n_dp) * self.n_rep + lax.rem(self.c + j, self.n_rep))
        self.slot(self.k)[...] = self.src[...]
        for copy in self.first():
            copy.wait_send()
        for _, group in self.second():
            for copy in group:
                copy.wait_send()


class LineGather:
    def __init__(self, buf, parts, send, recv, n_mp):
        self.buf, self.parts, self.send, self.recv, self.n_mp = buf, parts, send, recv, n_mp
        self.z = lax.axis_index("mp")

    def copy(self, m, h, way):
        i = m * self.parts + h
        return remote(self.buf.at[i], self.buf.at[i], self.send.at[way, i], self.recv.at[i],
                      {"mp": self.z + 2 * way - 1})

    def out(self, m, h, way, act):
        last = self.z < self.n_mp - 1 if way else self.z > 0

        @pl.when(last)
        def _():
            act(self.copy(m, h, way))

    def start(self):
        for h in range(self.parts):
            for way in (0, 1):
                self.out(self.z, h, way, lambda copy: copy.start())

    def take_left(self, m, h):
        self.copy(m, h, 1).wait_recv()
        self.out(m, h, 1, lambda copy: copy.start())

    def take_right(self, m, h):
        self.copy(m, h, 0).wait_recv()
        self.out(m, h, 0, lambda copy: copy.start())

    def step(self, s):
        for h in range(self.parts):
            @pl.when(self.z - s >= 0)
            def _():
                self.take_left(self.z - s, h)

            @pl.when(self.z + s < self.n_mp)
            def _():
                self.take_right(self.z + s, h)

    def finish(self):
        @pl.loop(0, self.n_mp)
        def _(m):
            for h in range(self.parts):
                @pl.when(m <= self.z)
                def _():
                    self.out(m, h, 1, lambda copy: copy.wait_send())

                @pl.when(m >= self.z)
                def _():
                    self.out(m, h, 0, lambda copy: copy.wait_send())


def turn_kernel(n_mp, n_dp, n_rep, fails, ids, counts, g_ref, a_ref, q_ref, basis_hbm, u_out, r_out, q_out,
                s_own, s_all, s_block, a_all, q_rows, q_cols, r_own, r_all, u_own, left, right,
                s_send, s_recv, a_send, a_recv, qr_send, qr_recv, qc_send, qc_recv, r_send, r_recv,
                ul_send, ul_recv, ur_send, ur_recv, basis_ref, basis_sem):
    load = pltpu.make_async_copy(basis_hbm, basis_ref, basis_sem)
    load.start()
    z = lax.axis_index("mp")
    greet(z_links(n_mp) + x_links(n_dp) + core_links(n_rep))
    s = PlaneGather(s_own, s_all, s_send, s_recv, n_dp, n_rep)
    qc = PlaneGather(q_ref, q_cols, qc_send, qc_recv, n_dp, n_rep)
    r = PlaneGather(r_own, r_all, r_send, r_recv, n_dp, n_rep)
    a = LineGather(a_all, 1, a_send, a_recv, n_mp)
    qr = LineGather(q_rows, 1, qr_send, qr_recv, n_mp)
    depth, width = a_ref.shape[1], q_ref.shape[1]
    wide = basis_ref.shape[1]
    rows = u_own.shape[0] // STEPS
    blocks = u_own.shape[0] // (s_block.shape[0] * LEN)
    per = STEPS // blocks
    tile = 256 if wide % 256 == 0 else wide

    a_all[z] = a_ref[...]
    a.start()

    @pl.loop(0, counts.shape[0])
    def _(i):
        count = jnp.full((LEN, 1), counts[i], jnp.int32)
        slot = lax.broadcasted_iota(jnp.int32, (LEN, 1), 0)
        weight = jnp.where(slot < count, 1.0 / count.astype(jnp.float32), 0.0)
        s_own[i] = (g_ref[i].astype(jnp.float32) * weight).astype(jnp.bfloat16)

    s.start()
    q_rows[z] = q_ref[...]
    a.step(1)
    qr.start()
    for i in range(2, n_mp):
        a.step(i)
    s.forward()
    qc.start()
    s.finish()
    load.wait()

    def at(i):
        return pl.ds(pl.multiple_of(i * rows, rows), rows)

    def copy(buf, i, send, recv, way):
        return remote(buf.at[at(i)], buf.at[at(i)], send.at[i], recv.at[i], {"mp": z + way})

    def take(buf, i, send, recv, way, first, last):
        @pl.when(first)
        def _():
            buf[at(i), :] = u_own[at(i), :]

        @pl.when(jnp.logical_not(first))
        def _():
            copy(buf, i, send, recv, way).wait_recv()
            buf[at(i), :] = (buf[at(i), :].astype(jnp.float32)
                             + u_own[at(i), :].astype(jnp.float32)).astype(jnp.bfloat16)

        @pl.when(jnp.logical_not(last))
        def _():
            copy(buf, i, send, recv, way).start()

    def turn(block):
        prompts = s_block.shape[0]

        @pl.loop(0, prompts)
        def _(i):
            s_block[i] = s_all[ids[block * prompts + i]]

        size = prompts * LEN
        here = pl.ds(pl.multiple_of(block * size, size), size)

        @pl.loop(0, wide // tile)
        def _(j):
            cols = pl.ds(pl.multiple_of(j * tile, tile), tile)
            u_own[here, cols] = jnp.dot(
                s_block[...].reshape(size, s_block.shape[2]), basis_ref[:, cols],
                preferred_element_type=jnp.float32).astype(jnp.bfloat16)

    def rotate():
        qc.finish()
        total = jnp.zeros((a_ref.shape[0], width), jnp.float32)
        total = lax.fori_loop(
            0, n_mp,
            lambda m, t: t + jnp.dot(a_all[m], q_cols[pl.ds(pl.multiple_of(m * depth, depth), depth), :],
                                     preferred_element_type=jnp.float32),
            total)
        r_own[...] = total.astype(jnp.bfloat16).reshape(r_own.shape)
        r.start()

    @pl.loop(0, STEPS + LAG * (n_mp - 1))
    def _(t):
        @pl.when((t < STEPS) & (t % per == 0))
        def _():
            turn(t // per)

        i = t - LAG * z
        j = t - LAG * (n_mp - 1 - z)

        @pl.when((i >= 0) & (i < STEPS))
        def _():
            take(left, i, ul_send, ul_recv, 1, z == 0, z == n_mp - 1)

        @pl.when((j >= 0) & (j < STEPS))
        def _():
            take(right, j, ur_send, ur_recv, -1, z == n_mp - 1, z == 0)

        for n in range(1, n_mp):
            @pl.when(t == (n - 1) * STEPS // (n_mp - 1))
            def _():
                qr.step(n)

        @pl.when(t == STEPS // 2)
        def _():
            qc.forward()

        @pl.when(t == 3 * STEPS // 4)
        def _():
            rotate()

        @pl.when(t == STEPS)
        def _():
            r.forward()

    @pl.loop(0, STEPS)
    def _(i):
        u_out[at(i), :] = (left[at(i), :].astype(jnp.float32) + right[at(i), :].astype(jnp.float32)
                           - u_own[at(i), :].astype(jnp.float32)).astype(jnp.bfloat16)

        @pl.when(z < n_mp - 1)
        def _():
            copy(left, i, ul_send, ul_recv, 1).wait_send()

        @pl.when(z > 0)
        def _():
            copy(right, i, ur_send, ur_recv, -1).wait_send()

    r.finish()

    @pl.loop(0, fails)
    def _(i):
        r_out[i] = r_all[ids[i]]

    @pl.loop(0, n_mp)
    def _(m):
        q_out[:, pl.ds(pl.multiple_of(m * width, width), width)] = q_rows[m]

    a.finish()
    qr.finish()


def back_kernel(n_mp, n_dp, n_rep, parts, d_ref, g_hbm, q_ref, out_ref, back, held, part, other, across,
                z_send, z_recv, c_send, c_recv, x_send, x_recv, o_send, o_recv, g_ref, g_sem):
    load = pltpu.make_async_copy(g_hbm, g_ref, g_sem)
    load.start()
    z, x, c = lax.axis_index("mp"), lax.axis_index("dp"), lax.axis_index("rep")
    greet(z_links(n_mp) + x_links(n_dp) + core_links(n_rep))
    n = n_mp * parts
    rows, width = held.shape[1], held.shape[2]
    half = rows // n_rep
    tile = next(t for t in (256, 128, 64, 32, 16) if rows % t == 0)
    small = next(t for t in (128, 64, 32, 16) if half % t == 0)
    core = {"rep": 1 - c}
    mine = pl.ds(pl.multiple_of(c * half, half), half)
    theirs = pl.ds(pl.multiple_of((1 - c) * half, half), half)
    line = LineGather(held, parts, z_send, z_recv, n_mp)

    for h in range(parts):
        held[z * parts + h] = d_ref[:, h * width:(h + 1) * width]
    line.start()

    low, high = z, n_mp - 1 - z
    near = jnp.minimum(low, high)
    both = 2 * near * parts

    def place(p):
        q = p - parts
        pair, turn = q // (2 * parts), q % (2 * parts)
        far = q - both
        is_pair = q < both
        s = jnp.where(is_pair, pair + 1, near + far // parts + 1)
        h = jnp.where(is_pair, turn // 2, far % parts)
        from_left = jnp.where(is_pair, turn % 2 == 0, low > high)
        own = p < parts
        m = jnp.where(own, z, jnp.where(from_left, z - s, z + s))
        return m, jnp.where(own, p, h), own, from_left

    def columns(p):
        m, h, _, _ = place(p)
        return pl.ds(pl.multiple_of((m * parts + h) * width, width), width)

    def core_copy(p):
        return remote(part.at[p, theirs], other.at[p], c_send.at[p], c_recv.at[p], core)

    def x_copies(p):
        return [remote(part.at[p, mine], across.at[p, i - 1], x_send.at[p, i - 1], x_recv.at[p, i - 1],
                       {"dp": lax.rem(x + i, n_dp)}) for i in range(1, n_dp)]

    def out_copy(p, whose):
        return remote(back.at[whose, columns(p)], back.at[whose, columns(p)], o_send.at[p], o_recv.at[p], core)

    def multiply(p):
        m, h, own, from_left = place(p)

        @pl.when(jnp.logical_not(own) & from_left)
        def _():
            line.take_left(m, h)

        @pl.when(jnp.logical_not(own) & jnp.logical_not(from_left))
        def _():
            line.take_right(m, h)

        @pl.loop(0, rows // tile)
        def _(t):
            at = pl.ds(pl.multiple_of(t * tile, tile), tile)
            part[p, at, :] = jnp.dot(
                g_ref[at, :], held[m * parts + h], preferred_element_type=jnp.float32).astype(jnp.bfloat16)

        core_copy(p).start()

    def add_cores(p):
        core_copy(p).wait()

        @pl.loop(0, half // small)
        def _(t):
            here = pl.ds(pl.multiple_of(c * half + t * small, small), small)
            at = pl.ds(pl.multiple_of(t * small, small), small)
            part[p, here, :] = (part[p, here, :].astype(jnp.float32)
                                + other[p, at, :].astype(jnp.float32)).astype(jnp.bfloat16)

        for copy in x_copies(p):
            copy.start()

    def add_chips(p):
        for copy in x_copies(p):
            copy.wait()

        @pl.loop(0, half // small)
        def _(t):
            here = pl.ds(pl.multiple_of(c * half + t * small, small), small)
            at = pl.ds(pl.multiple_of(t * small, small), small)
            total = part[p, here, :].astype(jnp.float32)
            for i in range(n_dp - 1):
                total += across[p, i, at, :].astype(jnp.float32)
            back[here, columns(p)] = total.astype(jnp.bfloat16)

        out_copy(p, mine).start()

    def finish(p):
        out_copy(p, theirs).wait_recv()
        cols = columns(p)

        @pl.loop(0, rows // tile)
        def _(t):
            at = pl.ds(pl.multiple_of(t * tile, tile), tile)
            out_ref[at, :] += lax.dot_general(
                back[at, cols], q_ref[:, cols], (((1,), (1,)), ((), ())), preferred_element_type=jnp.float32)

    out_ref[...] = jnp.zeros_like(out_ref)
    load.wait()

    @pl.loop(0, n + 2)
    def _(t):
        @pl.when(t < n)
        def _():
            multiply(t)

        @pl.when((t >= 1) & (t < n + 1))
        def _():
            add_chips(t - 1)

        @pl.when(t >= 2)
        def _():
            finish(t - 2)

        @pl.when(t < n)
        def _():
            add_cores(t)

    @pl.loop(0, n)
    def _(p):
        out_copy(p, mine).wait_send()

    line.finish()


def shards(n_mp, n_dp, n_rep, activations, out_grads, basis_grad, basis_act, eigen_values, token_counts, fail_ids):
    tokens, features = activations.shape
    hidden = out_grads.shape[1]
    wide = basis_grad.shape[1]
    rows = basis_act.shape[0]
    planes = n_dp * n_rep
    fails = fail_ids.shape[0]
    prompts = token_counts.shape[0]
    live = fails * LEN
    bf16 = jnp.bfloat16
    dma = pltpu.SemaphoreType.DMA
    vmem = pl.BlockSpec(memory_space=pltpu.VMEM)
    sends = n_dp + n_rep - 2 + (n_dp - 1) * (n_rep - 1)
    plane_sems = [dma((sends,)), dma((planes,))]
    line_sems = [dma((2, n_mp)), dma((n_mp,))]
    smem = pl.BlockSpec(memory_space=pltpu.SMEM)
    blocks = next(b for b in (4, 2, 1) if fails % b == 0 and STEPS % b == 0)
    turned, rotated, basis_rows = pl.pallas_call(
        functools.partial(turn_kernel, n_mp, n_dp, n_rep, fails),
        out_shape=(
            jax.ShapeDtypeStruct((live, wide), bf16),
            jax.ShapeDtypeStruct((fails, LEN, features), bf16),
            jax.ShapeDtypeStruct((rows, n_mp * features), bf16),
        ),
        in_specs=[smem, smem, vmem, vmem, vmem, pl.BlockSpec(memory_space=pl.ANY)],
        out_specs=(vmem, vmem, vmem),
        scratch_shapes=[
            pltpu.VMEM((prompts, LEN, hidden), bf16),
            pltpu.VMEM((planes * prompts, LEN, hidden), bf16),
            pltpu.VMEM((fails // blocks, LEN, hidden), bf16),
            pltpu.VMEM((n_mp, tokens, features), bf16),
            pltpu.VMEM((n_mp, rows, features), bf16),
            pltpu.VMEM((planes * rows, features), bf16),
            pltpu.VMEM((prompts, LEN, features), bf16),
            pltpu.VMEM((planes * prompts, LEN, features), bf16),
            pltpu.VMEM((live, wide), bf16),
            pltpu.VMEM((live, wide), bf16),
            pltpu.VMEM((live, wide), bf16),
        ] + plane_sems + line_sems + line_sems + plane_sems + plane_sems + [dma((STEPS,))] * 4 + [pltpu.VMEM(basis_grad.shape, bf16), dma],
        compiler_params=pltpu.CompilerParams(
            collective_id=0, has_side_effects=True, vmem_limit_bytes=VMEM_LIMIT),
        name="turn_grads",
    )(fail_ids, token_counts, out_grads.reshape(prompts, LEN, hidden), activations, basis_act, basis_grad)
    rotated = rotated.reshape(live, features)

    eigen_grad = lax.dot_general(
        turned, rotated, (((0,), (0,)), ((), ())), preferred_element_type=jnp.float32)
    damped = (eigen_grad / (eigen_values + DAMPING)).astype(bf16)

    parts = max(1, features // 256)
    width = features // parts
    n = n_mp * parts
    half = hidden // n_rep
    return pl.pallas_call(
        functools.partial(back_kernel, n_mp, n_dp, n_rep, parts),
        out_shape=jax.ShapeDtypeStruct((hidden, rows), jnp.float32),
        in_specs=[vmem, pl.BlockSpec(memory_space=pl.ANY), vmem],
        out_specs=vmem,
        scratch_shapes=[
            pltpu.VMEM((hidden, n_mp * features), bf16),
            pltpu.VMEM((n, wide, width), bf16),
            pltpu.VMEM((n, hidden, width), bf16),
            pltpu.VMEM((n, half, width), bf16),
            pltpu.VMEM((n, n_dp - 1, half, width), bf16),
            dma((2, n)), dma((n,)),
            dma((n,)), dma((n,)),
            dma((n, n_dp - 1)), dma((n, n_dp - 1)),
            dma((n,)), dma((n,)),
            pltpu.VMEM(basis_grad.shape, bf16), dma,
        ],
        compiler_params=pltpu.CompilerParams(
            collective_id=1, has_side_effects=True, vmem_limit_bytes=VMEM_LIMIT),
        name="back_rotate",
    )(damped, basis_grad, basis_rows)


def solution(mesh):
    return jax.shard_map(
        functools.partial(shards, mesh.shape["mp"], mesh.shape["dp"], mesh.shape["rep"]),
        mesh=mesh,
        in_specs=(
            P(("groups", "dp", "rep"), "mp"),
            P(("groups", "dp", "rep"), "mp"),
            P(("groups", "mp"), ("dp", "rep")),
            P(("groups", "dp", "rep"), "mp"),
            P(("groups", "dp", "rep"), "mp"),
            P(("groups", "dp", "rep")),
            P("groups"),
        ),
        out_specs=P(("groups", "mp"), ("dp", "rep")),
        check_vma=False,
    )
```

```python
import functools

import jax
import jax.numpy as jnp
from jax import lax
from jax.experimental import pallas as pl
from jax.experimental.pallas import tpu as pltpu
from jax.sharding import PartitionSpec as P

LEN = 32
DAMPING = 0.25
STEPS = 24
LAG = 2
PART = 128
MESH = pl.DeviceIdType.MESH
VMEM_LIMIT = 60 * 1024 * 1024


def remote(src, dst, send, recv, where):
    return pltpu.make_async_remote_copy(
        src_ref=src, dst_ref=dst, send_sem=send, recv_sem=recv, device_id=where, device_id_type=MESH
    )


def when(there, act):
    if there is True:
        act()
    else:
        pl.when(there)(act)


def z_links(n_mp):
    z = lax.axis_index("mp")
    return [(z > 0, {"mp": z - 1}), (z < n_mp - 1, {"mp": z + 1})]


def x_links(n_dp):
    x = lax.axis_index("dp")
    return [(True, {"dp": lax.rem(x + i, n_dp)}) for i in range(1, n_dp)]


def core_links(n_rep):
    c = lax.axis_index("rep")
    return [(True, {"rep": lax.rem(c + i, n_rep)}) for i in range(1, n_rep)]


def greet(links):
    barrier = pltpu.get_barrier_semaphore()
    for there, where in links:
        when(there, lambda where=where: pl.semaphore_signal(
            barrier, inc=1, device_id=where, device_id_type=MESH))
    pl.semaphore_wait(barrier, sum(1 if there is True else there.astype(jnp.int32) for there, _ in links))


class PlaneGather:
    def __init__(self, src, buf, send, recv, n_dp, n_rep):
        self.src, self.buf, self.send, self.recv = src, buf, send, recv
        self.n_dp, self.n_rep = n_dp, n_rep
        self.rows = src.shape[0]
        self.x, self.c = lax.axis_index("dp"), lax.axis_index("rep")
        self.k = self.x * n_rep + self.c

    def slot(self, k):
        return self.buf.at[pl.ds(pl.multiple_of(k * self.rows, self.rows), self.rows)]

    def first(self):
        out = []
        for n, where in enumerate(w for _, w in x_links(self.n_dp) + core_links(self.n_rep)):
            out.append(remote(self.src, self.slot(self.k), self.send.at[n], self.recv.at[self.k], where))
        return out

    def second(self):
        out = []
        n = self.n_dp + self.n_rep - 2
        for i in range(1, self.n_dp):
            k = lax.rem(self.x + i, self.n_dp) * self.n_rep + self.c
            group = []
            for _, where in core_links(self.n_rep):
                group.append(remote(self.slot(k), self.slot(k), self.send.at[n], self.recv.at[k], where))
                n += 1
            out.append((k, group))
        return out

    def arrive(self, k):
        remote(self.slot(k), self.slot(k), self.send.at[0], self.recv.at[k], {"rep": self.c}).wait_recv()

    def start(self):
        for copy in self.first():
            copy.start()

    def forward(self):
        for k, group in self.second():
            self.arrive(k)
            for copy in group:
                copy.start()

    def finish(self):
        for i in range(self.n_dp):
            for j in range(1, self.n_rep):
                self.arrive(lax.rem(self.x + i, self.n_dp) * self.n_rep + lax.rem(self.c + j, self.n_rep))
        self.slot(self.k)[...] = self.src[...]
        for copy in self.first():
            copy.wait_send()
        for _, group in self.second():
            for copy in group:
                copy.wait_send()


class LineGather:
    def __init__(self, buf, parts, send, recv, n_mp):
        self.buf, self.parts, self.send, self.recv, self.n_mp = buf, parts, send, recv, n_mp
        self.z = lax.axis_index("mp")

    def copy(self, m, h, way):
        i = m * self.parts + h
        return remote(self.buf.at[i], self.buf.at[i], self.send.at[way, i], self.recv.at[i],
                      {"mp": self.z + 2 * way - 1})

    def out(self, m, h, way, act):
        last = self.z < self.n_mp - 1 if way else self.z > 0

        @pl.when(last)
        def _():
            act(self.copy(m, h, way))

    def start(self):
        for h in range(self.parts):
            for way in (0, 1):
                self.out(self.z, h, way, lambda copy: copy.start())

    def take_left(self, m, h):
        self.copy(m, h, 1).wait_recv()
        self.out(m, h, 1, lambda copy: copy.start())

    def take_right(self, m, h):
        self.copy(m, h, 0).wait_recv()
        self.out(m, h, 0, lambda copy: copy.start())

    def step(self, s):
        for h in range(self.parts):
            @pl.when(self.z - s >= 0)
            def _():
                self.take_left(self.z - s, h)

            @pl.when(self.z + s < self.n_mp)
            def _():
                self.take_right(self.z + s, h)

    def finish(self):
        @pl.loop(0, self.n_mp)
        def _(m):
            for h in range(self.parts):
                @pl.when(m <= self.z)
                def _():
                    self.out(m, h, 1, lambda copy: copy.wait_send())

                @pl.when(m >= self.z)
                def _():
                    self.out(m, h, 0, lambda copy: copy.wait_send())


def turn_kernel(n_mp, n_dp, n_rep, fails, ids, counts, g_ref, a_ref, q_ref, basis_hbm, u_out, r_out, q_rows,
                s_own, s_all, s_block, a_all, q_cols, r_own, r_all, u_own, left, right,
                s_send, s_recv, a_send, a_recv, qr_send, qr_recv, qc_send, qc_recv, r_send, r_recv,
                ul_send, ul_recv, ur_send, ur_recv, basis_ref, basis_sem):
    load = pltpu.make_async_copy(basis_hbm, basis_ref, basis_sem)
    load.start()
    z = lax.axis_index("mp")
    greet(z_links(n_mp) + x_links(n_dp) + core_links(n_rep))
    s = PlaneGather(s_own, s_all, s_send, s_recv, n_dp, n_rep)
    qc = PlaneGather(q_ref, q_cols, qc_send, qc_recv, n_dp, n_rep)
    r = PlaneGather(r_own, r_all, r_send, r_recv, n_dp, n_rep)
    a = LineGather(a_all, 1, a_send, a_recv, n_mp)
    qr = LineGather(q_rows, 1, qr_send, qr_recv, n_mp)
    depth, width = a_ref.shape[1], q_ref.shape[1]
    wide = basis_ref.shape[1]
    rows = u_own.shape[0] // STEPS
    blocks = u_own.shape[0] // (s_block.shape[0] * LEN)
    per = STEPS // blocks
    tile = 256 if wide % 256 == 0 else wide

    a_all[z] = a_ref[...]
    a.start()

    @pl.loop(0, counts.shape[0])
    def _(i):
        count = jnp.full((LEN, 1), counts[i], jnp.int32)
        slot = lax.broadcasted_iota(jnp.int32, (LEN, 1), 0)
        weight = jnp.where(slot < count, 1.0 / count.astype(jnp.float32), 0.0)
        s_own[i] = (g_ref[i].astype(jnp.float32) * weight).astype(jnp.bfloat16)

    s.start()
    q_rows[z] = q_ref[...]
    a.step(1)
    qr.start()
    for i in range(2, n_mp):
        a.step(i)
    s.forward()
    qc.start()
    s.finish()
    load.wait()

    def at(i):
        return pl.ds(pl.multiple_of(i * rows, rows), rows)

    def copy(buf, i, send, recv, way):
        return remote(buf.at[at(i)], buf.at[at(i)], send.at[i], recv.at[i], {"mp": z + way})

    def take(buf, i, send, recv, way, first, last):
        @pl.when(first)
        def _():
            buf[at(i), :] = u_own[at(i), :]

        @pl.when(jnp.logical_not(first))
        def _():
            copy(buf, i, send, recv, way).wait_recv()
            buf[at(i), :] = (buf[at(i), :].astype(jnp.float32)
                             + u_own[at(i), :].astype(jnp.float32)).astype(jnp.bfloat16)

        @pl.when(jnp.logical_not(last))
        def _():
            copy(buf, i, send, recv, way).start()

    def total(i):
        u_out[at(i), :] = (left[at(i), :].astype(jnp.float32) + right[at(i), :].astype(jnp.float32)
                           - u_own[at(i), :].astype(jnp.float32)).astype(jnp.bfloat16)

    def turn(block):
        prompts = s_block.shape[0]

        @pl.loop(0, prompts)
        def _(i):
            s_block[i] = s_all[ids[block * prompts + i]]

        size = prompts * LEN
        here = pl.ds(pl.multiple_of(block * size, size), size)

        @pl.loop(0, wide // tile)
        def _(j):
            cols = pl.ds(pl.multiple_of(j * tile, tile), tile)
            u_own[here, cols] = jnp.dot(
                s_block[...].reshape(size, s_block.shape[2]), basis_ref[:, cols],
                preferred_element_type=jnp.float32).astype(jnp.bfloat16)

    def rotate():
        qc.finish()
        product = lax.fori_loop(
            0, n_mp,
            lambda m, t: t + jnp.dot(a_all[m], q_cols[pl.ds(pl.multiple_of(m * depth, depth), depth), :],
                                     preferred_element_type=jnp.float32),
            jnp.zeros((a_ref.shape[0], width), jnp.float32))
        r_own[...] = product.astype(jnp.bfloat16).reshape(r_own.shape)
        r.start()

    @pl.loop(0, STEPS + LAG * (n_mp - 1))
    def _(t):
        @pl.when((t < STEPS) & (t % per == 0))
        def _():
            turn(t // per)

        i = t - LAG * z
        j = t - LAG * (n_mp - 1 - z)

        @pl.when((i >= 0) & (i < STEPS))
        def _():
            take(left, i, ul_send, ul_recv, 1, z == 0, z == n_mp - 1)

            @pl.when(z > n_mp - 1 - z)
            def _():
                total(i)

        @pl.when((j >= 0) & (j < STEPS))
        def _():
            take(right, j, ur_send, ur_recv, -1, z == n_mp - 1, z == 0)

            @pl.when(z <= n_mp - 1 - z)
            def _():
                total(j)

        for n in range(1, n_mp):
            @pl.when(t == (n - 1) * STEPS // (n_mp - 1))
            def _():
                qr.step(n)

        @pl.when(t == STEPS // 2)
        def _():
            qc.forward()

        @pl.when(t == 3 * STEPS // 4)
        def _():
            rotate()

        @pl.when(t == STEPS)
        def _():
            r.forward()

    @pl.loop(0, STEPS)
    def _(i):
        @pl.when(z < n_mp - 1)
        def _():
            copy(left, i, ul_send, ul_recv, 1).wait_send()

        @pl.when(z > 0)
        def _():
            copy(right, i, ur_send, ur_recv, -1).wait_send()

    r.finish()

    @pl.loop(0, fails)
    def _(i):
        r_out[i] = r_all[ids[i]]

    a.finish()
    qr.finish()


def back_kernel(n_mp, n_dp, n_rep, parts, u_ref, r_ref, e_ref, g_hbm, q_ref, out_ref, back, held, part, other, across,
                z_send, z_recv, c_send, c_recv, x_send, x_recv, o_send, o_recv, g_ref, g_sem):
    load = pltpu.make_async_copy(g_hbm, g_ref, g_sem)
    load.start()
    z, x, c = lax.axis_index("mp"), lax.axis_index("dp"), lax.axis_index("rep")
    greet(z_links(n_mp) + x_links(n_dp) + core_links(n_rep))
    n = n_mp * parts
    rows, width = held.shape[1], held.shape[2]
    half = rows // n_rep
    deep = 256 if rows % 256 == 0 else rows
    tile = next(t for t in (256, 128, 64, 32, 16) if rows % t == 0)
    small = next(t for t in (128, 64, 32, 16) if half % t == 0)
    core = {"rep": 1 - c}
    mine = pl.ds(pl.multiple_of(c * half, half), half)
    theirs = pl.ds(pl.multiple_of((1 - c) * half, half), half)
    line = LineGather(held, parts, z_send, z_recv, n_mp)

    for h in range(parts):
        @pl.loop(0, held.shape[1] // deep)
        def _(t):
            at = pl.ds(pl.multiple_of(t * deep, deep), deep)
            eigen_grad = lax.dot_general(
                u_ref[:, at], r_ref[:, h * width:(h + 1) * width], (((0,), (0,)), ((), ())),
                preferred_element_type=jnp.float32)
            held[z * parts + h, at, :] = (
                eigen_grad / (e_ref[at, h * width:(h + 1) * width] + DAMPING)).astype(jnp.bfloat16)

        for way in (0, 1):
            line.out(z, h, way, lambda copy: copy.start())

    low, high = z, n_mp - 1 - z
    near = jnp.minimum(low, high)
    both = 2 * near * parts

    def place(p):
        q = p - parts
        pair, turn = q // (2 * parts), q % (2 * parts)
        far = q - both
        is_pair = q < both
        s = jnp.where(is_pair, pair + 1, near + far // parts + 1)
        h = jnp.where(is_pair, turn // 2, far % parts)
        from_left = jnp.where(is_pair, turn % 2 == 0, low > high)
        own = p < parts
        m = jnp.where(own, z, jnp.where(from_left, z - s, z + s))
        return m, jnp.where(own, p, h), own, from_left

    def columns(p):
        m, h, _, _ = place(p)
        return pl.ds(pl.multiple_of((m * parts + h) * width, width), width)

    def core_copy(p):
        return remote(part.at[p, theirs], other.at[p], c_send.at[p], c_recv.at[p], core)

    def x_copies(p):
        return [remote(part.at[p, mine], across.at[p, i - 1], x_send.at[p, i - 1], x_recv.at[p, i - 1],
                       {"dp": lax.rem(x + i, n_dp)}) for i in range(1, n_dp)]

    def out_copy(p, whose):
        return remote(back.at[whose, columns(p)], back.at[whose, columns(p)], o_send.at[p], o_recv.at[p], core)

    def multiply(p):
        m, h, own, from_left = place(p)

        @pl.when(jnp.logical_not(own) & from_left)
        def _():
            line.take_left(m, h)

        @pl.when(jnp.logical_not(own) & jnp.logical_not(from_left))
        def _():
            line.take_right(m, h)

        @pl.loop(0, rows // tile)
        def _(t):
            at = pl.ds(pl.multiple_of(t * tile, tile), tile)
            part[p, at, :] = jnp.dot(
                g_ref[at, :], held[m * parts + h], preferred_element_type=jnp.float32).astype(jnp.bfloat16)

        core_copy(p).start()

    def add_cores(p):
        core_copy(p).wait()

        @pl.loop(0, half // small)
        def _(t):
            here = pl.ds(pl.multiple_of(c * half + t * small, small), small)
            at = pl.ds(pl.multiple_of(t * small, small), small)
            part[p, here, :] = (part[p, here, :].astype(jnp.float32)
                                + other[p, at, :].astype(jnp.float32)).astype(jnp.bfloat16)

        for copy in x_copies(p):
            copy.start()

    def add_chips(p):
        for copy in x_copies(p):
            copy.wait()

        @pl.loop(0, half // small)
        def _(t):
            here = pl.ds(pl.multiple_of(c * half + t * small, small), small)
            at = pl.ds(pl.multiple_of(t * small, small), small)
            total = part[p, here, :].astype(jnp.float32)
            for i in range(n_dp - 1):
                total += across[p, i, at, :].astype(jnp.float32)
            back[here, columns(p)] = total.astype(jnp.bfloat16)

        out_copy(p, mine).start()

    def finish(p):
        out_copy(p, theirs).wait_recv()
        cols = columns(p)
        m, h, _, _ = place(p)

        @pl.loop(0, rows // tile)
        def _(t):
            at = pl.ds(pl.multiple_of(t * tile, tile), tile)
            out_ref[at, :] += lax.dot_general(
                back[at, cols], q_ref[m, :, pl.ds(pl.multiple_of(h * width, width), width)], (((1,), (1,)), ((), ())), preferred_element_type=jnp.float32)

    out_ref[...] = jnp.zeros_like(out_ref)
    load.wait()

    @pl.loop(0, n + 2)
    def _(t):
        @pl.when(t < n)
        def _():
            multiply(t)

        @pl.when((t >= 1) & (t < n + 1))
        def _():
            add_chips(t - 1)

        @pl.when(t >= 2)
        def _():
            finish(t - 2)

        @pl.when(t < n)
        def _():
            add_cores(t)

    @pl.loop(0, n)
    def _(p):
        out_copy(p, mine).wait_send()

    line.finish()


def shards(n_mp, n_dp, n_rep, activations, out_grads, basis_grad, basis_act, eigen_values, token_counts, fail_ids):
    tokens, features = activations.shape
    hidden = out_grads.shape[1]
    wide = basis_grad.shape[1]
    rows = basis_act.shape[0]
    planes = n_dp * n_rep
    fails = fail_ids.shape[0]
    prompts = token_counts.shape[0]
    live = fails * LEN
    bf16 = jnp.bfloat16
    dma = pltpu.SemaphoreType.DMA
    vmem = pl.BlockSpec(memory_space=pltpu.VMEM)
    sends = n_dp + n_rep - 2 + (n_dp - 1) * (n_rep - 1)
    plane_sems = [dma((sends,)), dma((planes,))]
    line_sems = [dma((2, n_mp)), dma((n_mp,))]
    smem = pl.BlockSpec(memory_space=pltpu.SMEM)
    blocks = next(b for b in (4, 2, 1) if fails % b == 0 and STEPS % b == 0)
    turned, rotated, basis_rows = pl.pallas_call(
        functools.partial(turn_kernel, n_mp, n_dp, n_rep, fails),
        out_shape=(
            jax.ShapeDtypeStruct((live, wide), bf16),
            jax.ShapeDtypeStruct((fails, LEN, features), bf16),
            jax.ShapeDtypeStruct((n_mp, rows, features), bf16),
        ),
        in_specs=[smem, smem, vmem, vmem, vmem, pl.BlockSpec(memory_space=pl.ANY)],
        out_specs=(vmem, vmem, vmem),
        scratch_shapes=[
            pltpu.VMEM((prompts, LEN, hidden), bf16),
            pltpu.VMEM((planes * prompts, LEN, hidden), bf16),
            pltpu.VMEM((fails // blocks, LEN, hidden), bf16),
            pltpu.VMEM((n_mp, tokens, features), bf16),
            pltpu.VMEM((planes * rows, features), bf16),
            pltpu.VMEM((prompts, LEN, features), bf16),
            pltpu.VMEM((planes * prompts, LEN, features), bf16),
            pltpu.VMEM((live, wide), bf16),
            pltpu.VMEM((live, wide), bf16),
            pltpu.VMEM((live, wide), bf16),
        ] + plane_sems + line_sems + line_sems + plane_sems + plane_sems + [dma((STEPS,))] * 4 + [pltpu.VMEM(basis_grad.shape, bf16), dma],
        compiler_params=pltpu.CompilerParams(
            collective_id=0, has_side_effects=True, vmem_limit_bytes=VMEM_LIMIT),
        name="turn_grads",
    )(fail_ids, token_counts, out_grads.reshape(prompts, LEN, hidden), activations, basis_act, basis_grad)
    rotated = rotated.reshape(live, features)

    parts = max(1, features // PART)
    width = features // parts
    n = n_mp * parts
    half = hidden // n_rep
    return pl.pallas_call(
        functools.partial(back_kernel, n_mp, n_dp, n_rep, parts),
        out_shape=jax.ShapeDtypeStruct((hidden, rows), jnp.float32),
        in_specs=[vmem, vmem, vmem, pl.BlockSpec(memory_space=pl.ANY), vmem],
        out_specs=vmem,
        scratch_shapes=[
            pltpu.VMEM((hidden, n_mp * features), bf16),
            pltpu.VMEM((n, wide, width), bf16),
            pltpu.VMEM((n, hidden, width), bf16),
            pltpu.VMEM((n, half, width), bf16),
            pltpu.VMEM((n, n_dp - 1, half, width), bf16),
            dma((2, n)), dma((n,)),
            dma((n,)), dma((n,)),
            dma((n, n_dp - 1)), dma((n, n_dp - 1)),
            dma((n,)), dma((n,)),
            pltpu.VMEM(basis_grad.shape, bf16), dma,
        ],
        compiler_params=pltpu.CompilerParams(
            collective_id=1, has_side_effects=True, vmem_limit_bytes=VMEM_LIMIT),
        name="back_rotate",
    )(turned, rotated, eigen_values, basis_grad, basis_rows)


def solution(mesh):
    return jax.shard_map(
        functools.partial(shards, mesh.shape["mp"], mesh.shape["dp"], mesh.shape["rep"]),
        mesh=mesh,
        in_specs=(
            P(("groups", "dp", "rep"), "mp"),
            P(("groups", "dp", "rep"), "mp"),
            P(("groups", "mp"), ("dp", "rep")),
            P(("groups", "dp", "rep"), "mp"),
            P(("groups", "dp", "rep"), "mp"),
            P(("groups", "dp", "rep")),
            P("groups"),
        ),
        out_specs=P(("groups", "mp"), ("dp", "rep")),
        check_vma=False,
    )
```

```python
import functools

import jax
import jax.numpy as jnp
from jax import lax
from jax.experimental import pallas as pl
from jax.experimental.pallas import tpu as pltpu
from jax.sharding import PartitionSpec as P

LEN = 32
DAMPING = 0.25
STEPS = 24
LAG = 2
MESH = pl.DeviceIdType.MESH
VMEM_LIMIT = 60 * 1024 * 1024


def remote(src, dst, send, recv, where):
    return pltpu.make_async_remote_copy(
        src_ref=src, dst_ref=dst, send_sem=send, recv_sem=recv, device_id=where, device_id_type=MESH
    )


def when(there, act):
    if there is True:
        act()
    else:
        pl.when(there)(act)


def z_links(n_mp):
    z = lax.axis_index("mp")
    return [(z > 0, {"mp": z - 1}), (z < n_mp - 1, {"mp": z + 1})]


def x_links(n_dp):
    x = lax.axis_index("dp")
    return [(True, {"dp": lax.rem(x + i, n_dp)}) for i in range(1, n_dp)]


def core_links(n_rep):
    c = lax.axis_index("rep")
    return [(True, {"rep": lax.rem(c + i, n_rep)}) for i in range(1, n_rep)]


def greet(links):
    barrier = pltpu.get_barrier_semaphore()
    for there, where in links:
        when(there, lambda where=where: pl.semaphore_signal(
            barrier, inc=1, device_id=where, device_id_type=MESH))
    pl.semaphore_wait(barrier, sum(1 if there is True else there.astype(jnp.int32) for there, _ in links))


class PlaneGather:
    def __init__(self, src, buf, send, recv, n_dp, n_rep):
        self.src, self.buf, self.send, self.recv = src, buf, send, recv
        self.n_dp, self.n_rep = n_dp, n_rep
        self.rows = src.shape[0]
        self.x, self.c = lax.axis_index("dp"), lax.axis_index("rep")
        self.k = self.x * n_rep + self.c

    def slot(self, k):
        return self.buf.at[pl.ds(pl.multiple_of(k * self.rows, self.rows), self.rows)]

    def first(self):
        out = []
        for n, where in enumerate(w for _, w in x_links(self.n_dp) + core_links(self.n_rep)):
            out.append(remote(self.src, self.slot(self.k), self.send.at[n], self.recv.at[self.k], where))
        return out

    def second(self):
        out = []
        n = self.n_dp + self.n_rep - 2
        for i in range(1, self.n_dp):
            k = lax.rem(self.x + i, self.n_dp) * self.n_rep + self.c
            group = []
            for _, where in core_links(self.n_rep):
                group.append(remote(self.slot(k), self.slot(k), self.send.at[n], self.recv.at[k], where))
                n += 1
            out.append((k, group))
        return out

    def arrive(self, k):
        remote(self.slot(k), self.slot(k), self.send.at[0], self.recv.at[k], {"rep": self.c}).wait_recv()

    def start(self):
        for copy in self.first():
            copy.start()

    def forward(self):
        for k, group in self.second():
            self.arrive(k)
            for copy in group:
                copy.start()

    def finish(self):
        for i in range(self.n_dp):
            for j in range(1, self.n_rep):
                self.arrive(lax.rem(self.x + i, self.n_dp) * self.n_rep + lax.rem(self.c + j, self.n_rep))
        self.slot(self.k)[...] = self.src[...]
        for copy in self.first():
            copy.wait_send()
        for _, group in self.second():
            for copy in group:
                copy.wait_send()


class LineGather:
    def __init__(self, buf, parts, send, recv, n_mp):
        self.buf, self.parts, self.send, self.recv, self.n_mp = buf, parts, send, recv, n_mp
        self.z = lax.axis_index("mp")

    def copy(self, m, h, way):
        i = m * self.parts + h
        return remote(self.buf.at[i], self.buf.at[i], self.send.at[way, i], self.recv.at[i],
                      {"mp": self.z + 2 * way - 1})

    def out(self, m, h, way, act):
        last = self.z < self.n_mp - 1 if way else self.z > 0

        @pl.when(last)
        def _():
            act(self.copy(m, h, way))

    def start(self):
        for h in range(self.parts):
            for way in (0, 1):
                self.out(self.z, h, way, lambda copy: copy.start())

    def take_left(self, m, h):
        self.copy(m, h, 1).wait_recv()
        self.out(m, h, 1, lambda copy: copy.start())

    def take_right(self, m, h):
        self.copy(m, h, 0).wait_recv()
        self.out(m, h, 0, lambda copy: copy.start())

    def step(self, s):
        for h in range(self.parts):
            @pl.when(self.z - s >= 0)
            def _():
                self.take_left(self.z - s, h)

            @pl.when(self.z + s < self.n_mp)
            def _():
                self.take_right(self.z + s, h)

    def finish(self):
        @pl.loop(0, self.n_mp)
        def _(m):
            for h in range(self.parts):
                @pl.when(m <= self.z)
                def _():
                    self.out(m, h, 1, lambda copy: copy.wait_send())

                @pl.when(m >= self.z)
                def _():
                    self.out(m, h, 0, lambda copy: copy.wait_send())


def turn_kernel(n_mp, n_dp, n_rep, fails, ids, counts, g_ref, a_ref, q_ref, basis_hbm, u_out, r_out, q_rows,
                s_own, s_all, s_block, a_all, q_cols, r_own, r_all, u_own, left, right,
                s_send, s_recv, a_send, a_recv, qr_send, qr_recv, qc_send, qc_recv, r_send, r_recv,
                ul_send, ul_recv, ur_send, ur_recv, basis_ref, basis_sem):
    load = pltpu.make_async_copy(basis_hbm, basis_ref, basis_sem)
    load.start()
    z = lax.axis_index("mp")
    greet(z_links(n_mp) + x_links(n_dp) + core_links(n_rep))
    s = PlaneGather(s_own, s_all, s_send, s_recv, n_dp, n_rep)
    qc = PlaneGather(q_ref, q_cols, qc_send, qc_recv, n_dp, n_rep)
    r = PlaneGather(r_own, r_all, r_send, r_recv, n_dp, n_rep)
    a = LineGather(a_all, 1, a_send, a_recv, n_mp)
    qr = LineGather(q_rows, 1, qr_send, qr_recv, n_mp)
    depth, width = a_ref.shape[1], q_ref.shape[1]
    wide = basis_ref.shape[1]
    rows = u_own.shape[0] // STEPS
    blocks = u_own.shape[0] // (s_block.shape[0] * LEN)
    per = STEPS // blocks
    tile = 256 if wide % 256 == 0 else wide

    a_all[z] = a_ref[...]
    a.start()

    @pl.loop(0, counts.shape[0])
    def _(i):
        count = jnp.full((LEN, 1), counts[i], jnp.int32)
        slot = lax.broadcasted_iota(jnp.int32, (LEN, 1), 0)
        weight = jnp.where(slot < count, 1.0 / count.astype(jnp.float32), 0.0)
        s_own[i] = (g_ref[i].astype(jnp.float32) * weight).astype(jnp.bfloat16)

    s.start()
    q_rows[z] = q_ref[...]
    a.step(1)
    qr.start()
    for i in range(2, n_mp):
        a.step(i)
    s.forward()
    qc.start()
    s.finish()
    load.wait()

    def at(i):
        return pl.ds(pl.multiple_of(i * rows, rows), rows)

    def copy(buf, i, send, recv, way):
        return remote(buf.at[at(i)], buf.at[at(i)], send.at[i], recv.at[i], {"mp": z + way})

    def take(buf, i, send, recv, way, first, last):
        @pl.when(first)
        def _():
            buf[at(i), :] = u_own[at(i), :]

        @pl.when(jnp.logical_not(first))
        def _():
            copy(buf, i, send, recv, way).wait_recv()
            buf[at(i), :] = (buf[at(i), :].astype(jnp.float32)
                             + u_own[at(i), :].astype(jnp.float32)).astype(jnp.bfloat16)

        @pl.when(jnp.logical_not(last))
        def _():
            copy(buf, i, send, recv, way).start()

    def total(i):
        u_out[at(i), :] = (left[at(i), :].astype(jnp.float32) + right[at(i), :].astype(jnp.float32)
                           - u_own[at(i), :].astype(jnp.float32)).astype(jnp.bfloat16)

    def turn(block):
        prompts = s_block.shape[0]

        @pl.loop(0, prompts)
        def _(i):
            s_block[i] = s_all[ids[block * prompts + i]]

        size = prompts * LEN
        here = pl.ds(pl.multiple_of(block * size, size), size)

        @pl.loop(0, wide // tile)
        def _(j):
            cols = pl.ds(pl.multiple_of(j * tile, tile), tile)
            u_own[here, cols] = jnp.dot(
                s_block[...].reshape(size, s_block.shape[2]), basis_ref[:, cols],
                preferred_element_type=jnp.float32).astype(jnp.bfloat16)

    def rotate():
        qc.finish()
        product = lax.fori_loop(
            0, n_mp,
            lambda m, t: t + jnp.dot(a_all[m], q_cols[pl.ds(pl.multiple_of(m * depth, depth), depth), :],
                                     preferred_element_type=jnp.float32),
            jnp.zeros((a_ref.shape[0], width), jnp.float32))
        r_own[...] = product.astype(jnp.bfloat16).reshape(r_own.shape)
        r.start()

    @pl.loop(0, STEPS + LAG * (n_mp - 1))
    def _(t):
        @pl.when((t < STEPS) & (t % per == 0))
        def _():
            turn(t // per)

        i = t - LAG * z
        j = t - LAG * (n_mp - 1 - z)

        @pl.when((i >= 0) & (i < STEPS))
        def _():
            take(left, i, ul_send, ul_recv, 1, z == 0, z == n_mp - 1)

            @pl.when(z > n_mp - 1 - z)
            def _():
                total(i)

        @pl.when((j >= 0) & (j < STEPS))
        def _():
            take(right, j, ur_send, ur_recv, -1, z == n_mp - 1, z == 0)

            @pl.when(z <= n_mp - 1 - z)
            def _():
                total(j)

        for n in range(1, n_mp):
            @pl.when(t == min((n - 1) * STEPS // 4, STEPS + LAG * (n_mp - 1) - 1))
            def _():
                qr.step(n)

        @pl.when(t == STEPS // 2)
        def _():
            qc.forward()

        @pl.when(t == 3 * STEPS // 4)
        def _():
            rotate()

        @pl.when(t == STEPS)
        def _():
            r.forward()

    @pl.loop(0, STEPS)
    def _(i):
        @pl.when(z < n_mp - 1)
        def _():
            copy(left, i, ul_send, ul_recv, 1).wait_send()

        @pl.when(z > 0)
        def _():
            copy(right, i, ur_send, ur_recv, -1).wait_send()

    r.finish()

    @pl.loop(0, fails)
    def _(i):
        r_out[i] = r_all[ids[i]]

    a.finish()
    qr.finish()


def back_kernel(n_mp, n_dp, n_rep, parts, d_ref, g_hbm, q_ref, out_ref, back, held, part, other, across,
                z_send, z_recv, c_send, c_recv, x_send, x_recv, o_send, o_recv, g_ref, g_sem):
    load = pltpu.make_async_copy(g_hbm, g_ref, g_sem)
    load.start()
    z, x, c = lax.axis_index("mp"), lax.axis_index("dp"), lax.axis_index("rep")
    greet(z_links(n_mp) + x_links(n_dp) + core_links(n_rep))
    n = n_mp * parts
    rows, width = held.shape[1], held.shape[2]
    half = rows // n_rep
    tile = next(t for t in (256, 128, 64, 32, 16) if rows % t == 0)
    small = next(t for t in (128, 64, 32, 16) if half % t == 0)
    core = {"rep": 1 - c}
    mine = pl.ds(pl.multiple_of(c * half, half), half)
    theirs = pl.ds(pl.multiple_of((1 - c) * half, half), half)
    line = LineGather(held, parts, z_send, z_recv, n_mp)

    for h in range(parts):
        held[z * parts + h] = d_ref[:, h * width:(h + 1) * width]
    line.start()

    low, high = z, n_mp - 1 - z
    near = jnp.minimum(low, high)
    both = 2 * near * parts

    def place(p):
        q = p - parts
        pair, turn = q // (2 * parts), q % (2 * parts)
        far = q - both
        is_pair = q < both
        s = jnp.where(is_pair, pair + 1, near + far // parts + 1)
        h = jnp.where(is_pair, turn // 2, far % parts)
        from_left = jnp.where(is_pair, turn % 2 == 0, low > high)
        own = p < parts
        m = jnp.where(own, z, jnp.where(from_left, z - s, z + s))
        return m, jnp.where(own, p, h), own, from_left

    def columns(p):
        m, h, _, _ = place(p)
        return pl.ds(pl.multiple_of((m * parts + h) * width, width), width)

    def core_copy(p):
        return remote(part.at[p, theirs], other.at[p], c_send.at[p], c_recv.at[p], core)

    def x_copies(p):
        return [remote(part.at[p, mine], across.at[p, i - 1], x_send.at[p, i - 1], x_recv.at[p, i - 1],
                       {"dp": lax.rem(x + i, n_dp)}) for i in range(1, n_dp)]

    def out_copy(p, whose):
        return remote(back.at[whose, columns(p)], back.at[whose, columns(p)], o_send.at[p], o_recv.at[p], core)

    def multiply(p):
        m, h, own, from_left = place(p)

        @pl.when(jnp.logical_not(own) & from_left)
        def _():
            line.take_left(m, h)

        @pl.when(jnp.logical_not(own) & jnp.logical_not(from_left))
        def _():
            line.take_right(m, h)

        @pl.loop(0, rows // tile)
        def _(t):
            at = pl.ds(pl.multiple_of(t * tile, tile), tile)
            part[p, at, :] = jnp.dot(
                g_ref[at, :], held[m * parts + h], preferred_element_type=jnp.float32).astype(jnp.bfloat16)

        core_copy(p).start()

    def add_cores(p):
        core_copy(p).wait()

        @pl.loop(0, half // small)
        def _(t):
            here = pl.ds(pl.multiple_of(c * half + t * small, small), small)
            at = pl.ds(pl.multiple_of(t * small, small), small)
            part[p, here, :] = (part[p, here, :].astype(jnp.float32)
                                + other[p, at, :].astype(jnp.float32)).astype(jnp.bfloat16)

        for copy in x_copies(p):
            copy.start()

    def add_chips(p):
        for copy in x_copies(p):
            copy.wait()

        @pl.loop(0, half // small)
        def _(t):
            here = pl.ds(pl.multiple_of(c * half + t * small, small), small)
            at = pl.ds(pl.multiple_of(t * small, small), small)
            total = part[p, here, :].astype(jnp.float32)
            for i in range(n_dp - 1):
                total += across[p, i, at, :].astype(jnp.float32)
            back[here, columns(p)] = total.astype(jnp.bfloat16)

        out_copy(p, mine).start()

    def finish(p):
        out_copy(p, theirs).wait_recv()
        cols = columns(p)
        m, h, _, _ = place(p)

        @pl.loop(0, rows // tile)
        def _(t):
            at = pl.ds(pl.multiple_of(t * tile, tile), tile)
            out_ref[at, :] += lax.dot_general(
                back[at, cols], q_ref[m, :, pl.ds(pl.multiple_of(h * width, width), width)], (((1,), (1,)), ((), ())), preferred_element_type=jnp.float32)

    out_ref[...] = jnp.zeros_like(out_ref)
    load.wait()

    @pl.loop(0, n + 2)
    def _(t):
        @pl.when(t < n)
        def _():
            multiply(t)

        @pl.when((t >= 1) & (t < n + 1))
        def _():
            add_chips(t - 1)

        @pl.when(t >= 2)
        def _():
            finish(t - 2)

        @pl.when(t < n)
        def _():
            add_cores(t)

    @pl.loop(0, n)
    def _(p):
        out_copy(p, mine).wait_send()

    line.finish()


def shards(n_mp, n_dp, n_rep, activations, out_grads, basis_grad, basis_act, eigen_values, token_counts, fail_ids):
    tokens, features = activations.shape
    hidden = out_grads.shape[1]
    wide = basis_grad.shape[1]
    rows = basis_act.shape[0]
    planes = n_dp * n_rep
    fails = fail_ids.shape[0]
    prompts = token_counts.shape[0]
    live = fails * LEN
    bf16 = jnp.bfloat16
    dma = pltpu.SemaphoreType.DMA
    vmem = pl.BlockSpec(memory_space=pltpu.VMEM)
    sends = n_dp + n_rep - 2 + (n_dp - 1) * (n_rep - 1)
    plane_sems = [dma((sends,)), dma((planes,))]
    line_sems = [dma((2, n_mp)), dma((n_mp,))]
    smem = pl.BlockSpec(memory_space=pltpu.SMEM)
    blocks = next(b for b in (4, 2, 1) if fails % b == 0 and STEPS % b == 0)
    turned, rotated, basis_rows = pl.pallas_call(
        functools.partial(turn_kernel, n_mp, n_dp, n_rep, fails),
        out_shape=(
            jax.ShapeDtypeStruct((live, wide), bf16),
            jax.ShapeDtypeStruct((fails, LEN, features), bf16),
            jax.ShapeDtypeStruct((n_mp, rows, features), bf16),
        ),
        in_specs=[smem, smem, vmem, vmem, vmem, pl.BlockSpec(memory_space=pl.ANY)],
        out_specs=(vmem, vmem, vmem),
        scratch_shapes=[
            pltpu.VMEM((prompts, LEN, hidden), bf16),
            pltpu.VMEM((planes * prompts, LEN, hidden), bf16),
            pltpu.VMEM((fails // blocks, LEN, hidden), bf16),
            pltpu.VMEM((n_mp, tokens, features), bf16),
            pltpu.VMEM((planes * rows, features), bf16),
            pltpu.VMEM((prompts, LEN, features), bf16),
            pltpu.VMEM((planes * prompts, LEN, features), bf16),
            pltpu.VMEM((live, wide), bf16),
            pltpu.VMEM((live, wide), bf16),
            pltpu.VMEM((live, wide), bf16),
        ] + plane_sems + line_sems + line_sems + plane_sems + plane_sems + [dma((STEPS,))] * 4 + [pltpu.VMEM(basis_grad.shape, bf16), dma],
        compiler_params=pltpu.CompilerParams(
            collective_id=0, has_side_effects=True, vmem_limit_bytes=VMEM_LIMIT),
        name="turn_grads",
    )(fail_ids, token_counts, out_grads.reshape(prompts, LEN, hidden), activations, basis_act, basis_grad)
    rotated = rotated.reshape(live, features)

    eigen_grad = lax.dot_general(
        turned, rotated, (((0,), (0,)), ((), ())), preferred_element_type=jnp.float32)
    damped = (eigen_grad / (eigen_values + DAMPING)).astype(bf16)

    parts = max(1, features // 256)
    width = features // parts
    n = n_mp * parts
    half = hidden // n_rep
    return pl.pallas_call(
        functools.partial(back_kernel, n_mp, n_dp, n_rep, parts),
        out_shape=jax.ShapeDtypeStruct((hidden, rows), jnp.float32),
        in_specs=[vmem, pl.BlockSpec(memory_space=pl.ANY), vmem],
        out_specs=vmem,
        scratch_shapes=[
            pltpu.VMEM((hidden, n_mp * features), bf16),
            pltpu.VMEM((n, wide, width), bf16),
            pltpu.VMEM((n, hidden, width), bf16),
            pltpu.VMEM((n, half, width), bf16),
            pltpu.VMEM((n, n_dp - 1, half, width), bf16),
            dma((2, n)), dma((n,)),
            dma((n,)), dma((n,)),
            dma((n, n_dp - 1)), dma((n, n_dp - 1)),
            dma((n,)), dma((n,)),
            pltpu.VMEM(basis_grad.shape, bf16), dma,
        ],
        compiler_params=pltpu.CompilerParams(
            collective_id=1, has_side_effects=True, vmem_limit_bytes=VMEM_LIMIT),
        name="back_rotate",
    )(damped, basis_grad, basis_rows)


def solution(mesh):
    return jax.shard_map(
        functools.partial(shards, mesh.shape["mp"], mesh.shape["dp"], mesh.shape["rep"]),
        mesh=mesh,
        in_specs=(
            P(("groups", "dp", "rep"), "mp"),
            P(("groups", "dp", "rep"), "mp"),
            P(("groups", "mp"), ("dp", "rep")),
            P(("groups", "dp", "rep"), "mp"),
            P(("groups", "dp", "rep"), "mp"),
            P(("groups", "dp", "rep")),
            P("groups"),
        ),
        out_specs=P(("groups", "mp"), ("dp", "rep")),
        check_vma=False,
    )
```
